32 devices in a mesh: req: 8 (over z, y), tp: 4 (over x, core).
Axes of the slice: x: 2, y: 2, z: 4, core: 2. Of those that a mesh axis runs over, the one named last changes fastest.
Arguments:
- tokens: bfloat16 [64, 16, 1792], P('req'), may hold values from -6 to 6
- conv_edge: bfloat16 [64, 2, 1792], P('req'), may hold values from -6 to 6
- state_start: float32 [16, 1956864], P('tp', 'req'), may hold values from -60 to 60
- norm_start: float32 [16, 64, 273], P('tp', 'req'), may hold values from -200 to 200, as said below
- accepted: int32 [64], P('req'), may hold values from 0 to 16
- owner: int32 [64], P('req'), may hold values from 0 to 7, as said below
- attn_gain: float32 [1792], replicated, may hold values from 0.5 to 1.5
- conv_weight: float32 [3, 1792], replicated, may hold values from -3 to 3
- w_query: bfloat16 [1792, 256], P(None, 'tp'), may hold values from -0.125 to 0.125
- w_key: bfloat16 [1792, 256], P(None, 'tp'), may hold values from -0.125 to 0.125
- w_value: bfloat16 [1792, 1792], P('tp'), may hold values from -0.125 to 0.125
- w_out: bfloat16 [1792, 1792], P('tp'), may hold values from -0.125 to 0.125
- mlp_gain: float32 [1792], replicated, may hold values from 0.5 to 1.5
- w_gate: bfloat16 [1792, 2048], P(None, 'tp'), may hold values from -0.125 to 0.125
- w_up: bfloat16 [1792, 2048], P(None, 'tp'), may hold values from -0.125 to 0.125
- w_down: bfloat16 [2048, 1792], P('tp'), may hold values from -0.125 to 0.125
Outputs:
- hidden_out: bfloat16 [64, 16, 1792], P('req')
- kept_state: float32 [16, 3913728], P('tp', 'req')
- kept_norm: float32 [16, 128, 273], P('tp', 'req')
- kept_edge: bfloat16 [128, 2, 1792], P('req', None, 'tp')
The draws below stay inside these ranges and needn't reach their ends.
Inputs may be any that keep to these rules, and one draw needn't show every extreme that they name: The requests of one device go to one owner at most 2 times, and some device sends exactly 2 to one owner; an owner receives at most 16 requests in all, and some owner exactly 16. Each norm_start[h, r] is a sum of key features: c times [1, m, (m_i m_j + v_i delta_ij) / sqrt(2) for i then j] with a count c from 4 to 48 (its first entry), a mean m of 16 entries and v_i from 0.2 to 1, so that phi(u) . norm_start[h, r] >= c / 2 for every vector u.
All inputs are finite; a program needn't handle non-finite values.
Results may differ from the reference program's by a relative error of at most 0.015.
Values may be sent and summed in bfloat16 or wider, within the bound.
No kernel may reach another device: no remote copies, remote signals or barrier semaphores. Data moves between devices by JAX's collectives and lax.ppermute only.
A program may use at most 128 MiB of HBM per device.

```python
import math
import jax
import jax.numpy as jnp
from jax import lax

D = 1792
H = 16
FD = 16
DV = 112
F = 273
FF = 2048
DRAFT = 16
KC = 3
RD = 8
REQS = 64
CAP = 16
PAIR_CAP = 2
N_REQ = 8


def start_law(key):
    base = jax.random.fold_in(key, 101)
    key_count, key_centre, key_spread = jax.random.split(base, 3)
    counts = jnp.exp(jax.random.uniform(key_count, (REQS, H), jnp.float32, math.log(4.0), math.log(48.0)))
    centre = 0.5 * jax.random.truncated_normal(key_centre, -4.0, 4.0, (REQS, H, FD), jnp.float32)
    spread = jax.random.uniform(key_spread, (REQS, H, FD), jnp.float32, 0.2, 1.0)
    return (counts, centre, spread)


def draw_norm_start(key, part):
    counts, centre, spread = start_law(key)
    identity = (jnp.arange(FD)[:, None] == jnp.arange(FD)[None, :]).astype(jnp.float32)
    square = (centre[..., :, None] * centre[..., None, :] + spread[..., :, None] * identity) * math.sqrt(0.5)
    whole = jnp.concatenate([jnp.ones((REQS, H, 1), jnp.float32), centre, square.reshape(REQS, H, FD * FD)], axis=-1)
    return jnp.transpose(whole * counts[..., None], (1, 0, 2))


def draw_state_start(key, part):
    counts, centre, spread = start_law(key)
    noise = jax.random.truncated_normal(jax.random.fold_in(key, 202), -4.0, 4.0, (H, REQS, F, DV), jnp.float32)
    scaled = noise * (0.3 * counts).T[:, :, None, None]
    return scaled.reshape(H, REQS * F * DV)


def draw_owner(key, part):
    subkeys = jax.random.split(jax.random.fold_in(key, 303), 4)
    hottest = jax.random.randint(subkeys[0], (), 0, N_REQ)
    source_rank = jax.random.permutation(subkeys[1], N_REQ)
    marks = (jnp.arange(N_REQ) == hottest).astype(jnp.int32)
    others = jnp.argsort(marks, stable=True)[:N_REQ - 1]
    others = others[jax.random.permutation(subkeys[2], N_REQ - 1)]
    scores = jax.random.randint(subkeys[3], (N_REQ, RD), 0, 1 << 20) * RD + jnp.arange(RD)[None, :]
    position = jnp.argsort(jnp.argsort(scores, axis=1), axis=1)
    hot_count = jnp.clip(CAP - source_rank * PAIR_CAP, 0, PAIR_CAP)[:, None]
    cyclic = (source_rank[:, None] + position - hot_count) % (N_REQ - 1)
    chosen = jnp.where(position < hot_count, hottest, others[cyclic])
    return chosen.reshape(REQS).astype(jnp.int32)


def plant(drawn, stream_key, low, high):
    longest = drawn.shape.index(max(drawn.shape))
    spots = []
    for shift in (0, 1):
        where = [jax.random.randint(jax.random.fold_in(stream_key, axis), (), 0, length) for axis, length in enumerate(drawn.shape)]
        where[longest] = (where[longest] + shift) % drawn.shape[longest]
        spots.append(tuple(where))
    return drawn.at[spots[0]].set(low).at[spots[1]].set(high)


def shard_levels(stream_key, extent, cuts, least, largest):
    factor_of = 1.0
    for dim, shards_of in cuts:
        steps = jax.random.uniform(jax.random.fold_in(jax.random.fold_in(stream_key, 6), dim), (shards_of,), jnp.float32, least / len(cuts), largest / len(cuts))
        factor_of = factor_of * jnp.repeat(jnp.exp(steps), extent[dim] // shards_of).reshape((-1,) + (1,) * (len(extent) - 1 - dim))
    return factor_of


def centred(key, extent, deviation, most, cuts=(), kind=jnp.bfloat16):
    drawn = deviation * jax.random.normal(key, extent, jnp.float32)
    if cuts:
        drawn = drawn * shard_levels(key, extent, cuts, -0.22, 0.18)
    return jnp.clip(drawn, -most, most).astype(kind)


def setup_inputs(seed: int = 0) -> dict:
    streams_of = jax.random.split(jax.random.key(seed), 17)
    return {
        "tokens": centred(streams_of[0], (REQS, DRAFT, D), 1.0, 6.0, ((0, 8),)),
        "conv_edge": centred(streams_of[1], (REQS, KC - 1, D), 1.0, 6.0, ((0, 8),)),
        "state_start": draw_state_start(jax.random.fold_in(streams_of[16], 71), 0),
        "norm_start": draw_norm_start(jax.random.fold_in(streams_of[16], 71), 0),
        "accepted": plant(jax.random.randint(streams_of[4], (REQS,), 0, DRAFT + 1), jax.random.fold_in(streams_of[4], 1), 0, DRAFT).astype(jnp.int32),
        "owner": draw_owner(jax.random.fold_in(streams_of[16], 71), 0),
        "attn_gain": jnp.clip(1.0 + 0.1 * jax.random.normal(streams_of[6], (D,), jnp.float32), 0.5, 1.5),
        "conv_weight": centred(streams_of[7], (KC, D), 0.5, 3.0, (), jnp.float32),
        "w_query": centred(streams_of[8], (D, H * FD), D ** -0.5, 0.125, ((1, 4),)),
        "w_key": centred(streams_of[9], (D, H * FD), D ** -0.5, 0.125, ((1, 4),)),
        "w_value": centred(streams_of[10], (D, D), D ** -0.5, 0.125, ((0, 4),)),
        "w_out": centred(streams_of[11], (D, D), D ** -0.5, 0.125, ((0, 4),)),
        "mlp_gain": jnp.clip(1.0 + 0.1 * jax.random.normal(streams_of[12], (D,), jnp.float32), 0.5, 1.5),
        "w_gate": centred(streams_of[13], (D, FF), D ** -0.5, 0.125, ((1, 4),)),
        "w_up": centred(streams_of[14], (D, FF), D ** -0.5, 0.125, ((1, 4),)),
        "w_down": centred(streams_of[15], (FF, D), FF ** -0.5, 0.125, ((0, 4),)),
    }


def features(values, width):
    scaled = values * width ** (-0.25)
    leading = values.shape[:-1]
    square = (scaled[..., :, None] * scaled[..., None, :]).reshape(leading + (width * width,)) * math.sqrt(0.5)
    return jnp.concatenate([jnp.ones(leading + (1,), scaled.dtype), scaled, square], axis=-1)

def rms_scaled(row_block, gain_row):
    widened = row_block.astype(jnp.float32)
    return widened * lax.rsqrt(lax.optimization_barrier(jnp.mean(widened * widened, axis=-1, keepdims=True)) + 1e-05) * gain_row

def reference(tokens, conv_edge, state_start, norm_start, accepted, owner, attn_gain, conv_weight, w_query, w_key, w_value, w_out, mlp_gain, w_gate, w_up, w_down):
    highest = lax.Precision.HIGHEST
    state_four = state_start.reshape(H, REQS, F, DV)
    normed = rms_scaled(tokens, attn_gain).astype(jnp.bfloat16)
    padded = jnp.concatenate([conv_edge, normed], axis=1)
    normed_wide = normed.astype(jnp.float32)
    convolved = jnp.zeros(normed.shape, jnp.float32)
    for tap_index in range(KC):
        convolved = convolved + conv_weight[tap_index] * padded[:, tap_index:tap_index + DRAFT].astype(jnp.float32)
    mixed_rows = (normed_wide + convolved * jax.nn.sigmoid(normed_wide)).astype(jnp.bfloat16)
    flat_rows = mixed_rows.reshape(REQS * DRAFT, D)
    query_rows = jnp.dot(flat_rows, w_query, preferred_element_type=jnp.float32).astype(jnp.bfloat16)
    key_rows = jnp.dot(flat_rows, w_key, preferred_element_type=jnp.float32).astype(jnp.bfloat16)
    value_rows = lax.dot_general(flat_rows, w_value, (((1,), (1,)), ((), ())), preferred_element_type=jnp.float32).astype(jnp.bfloat16)
    query_features = features(query_rows.astype(jnp.float32).reshape(REQS, DRAFT, H, FD), FD)
    key_features = features(key_rows.astype(jnp.float32).reshape(REQS, DRAFT, H, FD), FD)
    value_wide = value_rows.astype(jnp.float32).reshape(REQS, DRAFT, H, DV)
    causal = jnp.arange(DRAFT)[:, None] >= jnp.arange(DRAFT)[None, :]

    def attend(item):
        row_index, query_one, key_one, value_one = item
        state_one = state_four[:, row_index]
        norm_one = norm_start[:, row_index]
        scores = jnp.einsum('thf,shf->hts', query_one, key_one, precision=highest)
        scores = jnp.where(causal[None], scores, 0.0)
        numerator = jnp.einsum('thf,hfd->thd', query_one, state_one, precision=highest)
        numerator = numerator + jnp.einsum('hts,shd->thd', scores, value_one, precision=highest)
        denominator = jnp.einsum('thf,hf->th', query_one, norm_one, precision=highest) + lax.optimization_barrier(jnp.sum(scores, axis=-1)).T
        return numerator / denominator[..., None]
    attended = lax.map(attend, (jnp.arange(REQS, dtype=jnp.int32), query_features, key_features, value_wide))
    merged = attended.astype(jnp.bfloat16).reshape(REQS * DRAFT, D)
    residual = tokens.reshape(REQS * DRAFT, D).astype(jnp.float32) + jnp.dot(merged, w_out, preferred_element_type=jnp.float32)
    second = rms_scaled(residual, mlp_gain).astype(jnp.bfloat16)
    gate_rows = jnp.dot(second, w_gate, preferred_element_type=jnp.float32)
    upward = jnp.dot(second, w_up, preferred_element_type=jnp.float32)
    hidden = (jax.nn.silu(gate_rows) * upward).astype(jnp.bfloat16)
    hidden_out = (residual + jnp.dot(hidden, w_down, preferred_element_type=jnp.float32)).astype(jnp.bfloat16).reshape(REQS, DRAFT, D)
    taken_mask = (jnp.arange(DRAFT)[None, :] < accepted[:, None]).astype(jnp.float32)
    edge_index = (accepted[:, None] + jnp.arange(KC - 1)[None, :]).astype(jnp.int32)
    chosen_edge = jnp.take_along_axis(padded, edge_index[:, :, None], axis=1)
    marked = (owner[:, None] == jnp.arange(N_REQ)[None, :]).astype(jnp.int32)
    slot_index = lax.optimization_barrier(jnp.sum((jnp.cumsum(marked, axis=0) - marked) * marked, axis=1)).astype(jnp.int32)
    target_rows = (owner * CAP + slot_index).astype(jnp.int32)
    source = jnp.zeros((N_REQ * CAP,), jnp.int32).at[target_rows].set(jnp.arange(REQS, dtype=jnp.int32))
    filled = jnp.zeros((N_REQ * CAP,), jnp.float32).at[target_rows].set(1.0)

    def keep(item):
        source_row, live = item
        state_sum = state_four[:, source_row] + jnp.einsum('t,thf,thd->hfd', taken_mask[source_row], key_features[source_row], value_wide[source_row], precision=highest)
        totals = norm_start[:, source_row] + jnp.einsum('t,thf->hf', taken_mask[source_row], key_features[source_row], precision=highest)
        return (state_sum * live, totals * live)
    kept_rows, kept_totals = lax.map(keep, (source, filled))
    kept_state = jnp.transpose(kept_rows, (1, 0, 2, 3)).reshape(H, N_REQ * CAP * F * DV)
    kept_norm = jnp.transpose(kept_totals, (1, 0, 2))
    kept_edge = (chosen_edge[source].astype(jnp.float32) * filled[:, None, None]).astype(jnp.bfloat16)
    return (hidden_out, kept_state, kept_norm, kept_edge)
```

```python
import functools
import math

import jax
import jax.numpy as jnp
import numpy as np
from jax import lax
from jax.experimental import pallas as pl
from jax.experimental.pallas import tpu as pltpu
from jax.sharding import PartitionSpec as P

FD = 16
DV = 112
F = 273
CAP = 16
EPSILON = 1e-05

SPAN = F * DV
LINES = 240
WIDE = 256
PHASES = 7
EXTRA = 16
BF16 = jnp.bfloat16
F32 = jnp.float32


def grid_of(count):
    narrow = 1
    for size in range(1, count + 1):
        if count % size == 0 and 2 * size * size <= count:
            narrow = size
    return count // narrow, narrow


def line_of(index):
    return (index * SPAN) // 128, (index * SPAN) % 128


@functools.lru_cache(None)
def tables():
    scale_two = 0.25 * math.sqrt(0.5)

    def feature(column, f, left, right, bias):
        if f == 0:
            bias[0, column] = bias[1, column] = bias[2, column] = 1.0
        elif f <= FD:
            left[f - 1, column] = 1.0
            bias[1, column] = 1.0
            bias[2, column] = 0.5
        elif f < F:
            left[(f - 1 - FD) // FD, column] = 1.0
            right[(f - 1 - FD) % FD, column] = 1.0
            bias[2, column] = scale_two

    def build(width, places):
        left, right = np.zeros((FD, width)), np.zeros((FD, width))
        bias = np.zeros((8, width), np.float32)
        for column, f in places:
            feature(column, f, left, right, bias)
        return np.concatenate([left, right], 1).astype(BF16), bias

    lined = [
        (part * WIDE + m, 8 * (m // PHASES) + m % PHASES + part)
        for part in range(2)
        for m in range(LINES)
    ]
    line_pick, line_bias = build(2 * WIDE, lined)
    plain_pick, plain_bias = build(384, [(f, f) for f in range(F)])
    phase_mask = np.zeros((8, WIDE))
    for k in range(PHASES):
        phase_mask[k, k::PHASES] = 1.0
    turn = np.zeros((DV, PHASES * 128))
    for k in range(PHASES):
        for lane in range(128):
            turn[(16 * k + lane) % DV, 128 * k + lane] = 1.0
    return (
        line_pick,
        line_bias,
        plain_pick,
        plain_bias,
        phase_mask.astype(BF16),
        turn.astype(BF16),
    )


def dot_nt(a, b):
    return lax.dot_general(a, b, (((1,), (1,)), ((), ())), preferred_element_type=F32)


def dot_tn(a, b):
    return lax.dot_general(a, b, (((0,), (0,)), ((), ())), preferred_element_type=F32)


def dot_nn(a, b):
    return jnp.dot(a, b, preferred_element_type=F32)


def expand(x, pick_ref, bias_ref):
    width = bias_ref.shape[1]
    both = dot_nn(x, pick_ref[...])
    left = both[:, :width] + bias_ref[0:1, :]
    right = both[:, width:] + bias_ref[1:2, :]
    return left * right * bias_ref[2:3, :]


def spread(phi, mask_ref):
    pieces = []
    for k in range(PHASES):
        chosen = mask_ref[k : k + 1, :]
        for part in range(2):
            pieces.append(phi[:, part * WIDE : (part + 1) * WIDE] * chosen)
    return jnp.concatenate(pieces, axis=0)


def pack_kernel(
    heads, shape, pair_cap, tp_size,
    owner_ref, accepted_ref, state_ref, tokens_ref, edge_ref, norm_ref, gain_ref, conv_ref,
    wq_ref, wk_ref, wv_ref, pick_ref, bias_ref, plain_pick_ref, plain_bias_ref, mask_ref, turn_ref,
    *rest,
):
    nz, ny = shape
    count = nz * ny
    pieces = rest[:count]
    q_ref, k_ref, v_ref, start_ref = rest[count : count + 4]
    flat, padded, mixed, phi, plain, turned, edges, extra, stage, state_sem, out_sem = rest[count + 4 :]
    requests = owner_ref.shape[0]
    steps = tokens_ref.shape[0] // requests
    body = heads * LINES
    lines = state_ref.shape[0]
    loads = [
        pltpu.make_async_copy(state_ref.at[:, h], flat.at[h, pl.ds(0, lines)], state_sem.at[h])
        for h in range(heads)
    ]
    for load in loads:
        load.start()

    here = lax.axis_index("req")
    tp_here = lax.axis_index("tp")
    row_here, column_here = here // ny, here % ny

    for lane in range(count * pair_cap):
        stage[lane, body : body + EXTRA, :] = jnp.zeros((EXTRA, 128), BF16)

    for r in range(requests):
        base = 24 * r
        wide = tokens_ref[steps * r : steps * (r + 1), :].astype(F32)
        mean = jnp.mean(wide * wide, axis=-1, keepdims=True)
        normed = (wide * lax.rsqrt(mean + EPSILON) * gain_ref[...]).astype(BF16).astype(F32)
        padded[base + 8 : base + 8 + steps, :] = normed
        padded[base : base + 8, :] = jnp.zeros((8, wide.shape[1]), F32)
        padded[base + 6 : base + 8, :] = edge_ref[r].astype(F32)
        convolved = conv_ref[2:3, :] * normed
        for tap in range(2):
            convolved = convolved + conv_ref[tap : tap + 1, :] * padded[base + 6 + tap : base + 6 + tap + steps, :]
        blend = normed + convolved / (1.0 + jnp.exp(-normed))
        mixed[steps * r : steps * (r + 1), :] = blend.astype(BF16)

    queries = dot_nt(mixed[...], wq_ref[...]).astype(BF16)
    keys = dot_nt(mixed[...], wk_ref[...]).astype(BF16)
    values = dot_nt(mixed[...], wv_ref[...]).astype(BF16)
    q_ref[...] = queries
    k_ref[...] = keys
    v_ref[...] = values

    for h in range(heads):
        key = keys[:, FD * h : FD * (h + 1)]
        phi[h] = expand(key, pick_ref, bias_ref)
        plain[h] = expand(key, plain_pick_ref, plain_bias_ref)
        turned[h] = dot_nn(values[:, DV * h : DV * (h + 1)], turn_ref[...]).astype(BF16)

    column_width = tokens_ref.shape[1] // tp_size
    edge_rows = lax.broadcasted_iota(jnp.int32, (2 * requests, 24 * requests), 0)
    edge_columns = lax.broadcasted_iota(jnp.int32, (2 * requests, 24 * requests), 1)
    wanted = jnp.zeros(edge_rows.shape, jnp.int32)
    for r in range(requests):
        wanted = jnp.where(edge_rows // 2 == r, 24 * r + 6 + accepted_ref[r] + edge_rows % 2, wanted)
    choose = (edge_columns == wanted).astype(F32).astype(BF16)
    for i in range(tp_size):
        @pl.when(tp_here == i)
        def _():
            window = padded[:, column_width * i : column_width * (i + 1)].astype(BF16)
            edges[:, :column_width] = dot_nn(choose, window)

    lane_ids = lax.broadcasted_iota(jnp.int32, (LINES, 128), 1)
    one_line = lax.broadcasted_iota(jnp.int32, (EXTRA, 128), 1)
    one_row = lax.broadcasted_iota(jnp.int32, (EXTRA, 128), 0)
    step_ids = lax.broadcasted_iota(jnp.int32, (steps, 1), 0)
    edge_lines = -(-column_width // 128)
    for load in loads:
        load.wait()
    for r in range(requests):
        owner = owner_ref[r]
        rank = jnp.int32(0)
        for earlier in range(r):
            rank = rank + (owner_ref[earlier] == owner).astype(jnp.int32)
        far = lax.rem(owner // ny - row_here + nz, nz) * ny + lax.rem(owner % ny - column_here + ny, ny)
        lane = far * pair_cap + rank
        taken = (step_ids < accepted_ref[r]).astype(F32)
        first, shift = line_of(r)
        extra[...] = jnp.zeros((EXTRA, 128), F32)
        for h in range(heads):
            rows = slice(steps * r, steps * (r + 1))
            spread_keys = spread((phi[h, rows, :] * taken).astype(BF16), mask_ref)
            value_rows = turned[h, rows, :]
            parts = []
            for k in range(PHASES):
                block = value_rows[:, 128 * k : 128 * (k + 1)]
                early = one_line < DV - 16 * k
                zero = jnp.zeros((steps, 128), BF16)
                parts.append(jnp.where(early, block, zero))
                parts.append(jnp.where(early, zero, block))
            added = dot_tn(spread_keys, jnp.concatenate(parts, axis=0))[:LINES]
            start = flat[h, first : first + LINES, :]
            if shift:
                following = flat[h, first + 1 : first + 1 + LINES, :]
                start = pltpu.roll(jnp.where(lane_ids >= shift, start, following), 128 - shift, 1)
            start_ref[r, h] = start.astype(BF16)
            kept = start + added
            sums = jnp.sum(plain[h, rows, :] * taken, axis=0, keepdims=True)[:, :F] + norm_ref[h, r : r + 1, :]
            extra[2 * h : 2 * h + 1, :] = sums[:, :128]
            extra[2 * h + 1 : 2 * h + 2, :] = sums[:, 128:256]
            tail = jnp.concatenate([sums[:, 256:], jnp.zeros((1, 128 - (F - 256)), F32)], axis=1)
            stage[lane, h * LINES : (h + 1) * LINES - 16, :] = kept[: LINES - 16].astype(BF16)
            stage[lane, (h + 1) * LINES - 16 : (h + 1) * LINES, :] = jnp.where(
                one_row == 15, tail, kept[LINES - 16 :]
            ).astype(BF16)
        for j in range(2):
            for c in range(edge_lines):
                end = min(column_width, 128 * (c + 1))
                line = 2 * heads + edge_lines * j + c
                extra[line : line + 1, : end - 128 * c] = edges[2 * r + j : 2 * r + j + 1, 128 * c : end]
        mark = (one_row == EXTRA - 1) & (one_line == 127)
        stage[lane, body : body + EXTRA, :] = jnp.where(mark, 1.0, extra[...]).astype(BF16)
    sends = [
        pltpu.make_async_copy(stage.at[pl.ds(pair_cap * i, pair_cap)], pieces[i], out_sem.at[i])
        for i in range(count)
    ]
    for send in sends:
        send.start()
    for send in sends:
        send.wait()


def attend_kernel(
    heads, core_bit,
    q_ref, k_ref, v_ref, start_ref, norm_ref, wo_ref, pick_ref, bias_ref, plain_pick_ref, plain_bias_ref, mask_ref,
    keep_ref, send_ref,
    attended, part,
):
    requests = start_ref.shape[0]
    rows_all = q_ref.shape[0]
    steps = rows_all // requests
    row_ids = lax.broadcasted_iota(jnp.int32, (rows_all, rows_all), 0)
    column_ids = lax.broadcasted_iota(jnp.int32, (rows_all, rows_all), 1)
    allowed = (row_ids // steps == column_ids // steps) & (row_ids >= column_ids)
    lane_ids = lax.broadcasted_iota(jnp.int32, (steps, 128), 1)
    for h in range(heads):
        query = q_ref[:, FD * h : FD * (h + 1)]
        key = k_ref[:, FD * h : FD * (h + 1)]
        value = v_ref[:, DV * h : DV * (h + 1)]
        phi = expand(query, pick_ref, bias_ref).astype(BF16)
        plain = expand(query, plain_pick_ref, plain_bias_ref)
        inner = dot_nt(query, key) * 0.25
        scores = jnp.where(allowed, 1.0 + inner + 0.5 * inner * inner, 0.0)
        below = jnp.sum(scores, axis=-1, keepdims=True)
        within = dot_nn(scores.astype(BF16), value)
        for r in range(requests):
            rows = slice(steps * r, steps * (r + 1))
            spread_query = spread(phi[rows], mask_ref)[:, :LINES]
            lined = dot_nn(spread_query, start_ref[r, h])
            total = jnp.zeros((steps, 128), F32)
            for j in range(PHASES + 1):
                block = jnp.zeros((steps, 128), F32)
                if j < PHASES:
                    at = steps * (2 * j)
                    block = jnp.where(lane_ids < DV - 16 * j, lined[at : at + steps], 0.0)
                if j > 0:
                    at = steps * (2 * (j - 1) + 1)
                    block = jnp.where(lane_ids >= DV - 16 * (j - 1), lined[at : at + steps], block)
                total = total + (pltpu.roll(block, 16 * j, 1) if 0 < j < 8 else block)
            beneath = below[rows] + jnp.sum(plain[rows, :F] * norm_ref[h, r : r + 1, :], axis=-1, keepdims=True)
            attended[h, rows, :] = ((total[:, :DV] + within[rows]) / beneath).astype(BF16)
    out = dot_nn(attended[0], wo_ref[0:DV, :])
    for h in range(1, heads):
        out = out + dot_nn(attended[h], wo_ref[DV * h : DV * (h + 1), :])
    part[...] = out.astype(BF16)
    half = rows_all // 2
    mine = lax.rem(lax.axis_index("tp"), 2)
    keep_ref[...] = part[pl.ds(pl.multiple_of(mine * half, half), half), :]
    send_ref[...] = part[pl.ds(pl.multiple_of((1 - mine) * half, half), half), :]


def joined(own_ref, other_ref, scratch):
    half = own_ref.shape[0]
    mine = lax.rem(lax.axis_index("tp"), 2)
    scratch[pl.ds(pl.multiple_of(mine * half, half), half), :] = own_ref[...]
    scratch[pl.ds(pl.multiple_of((1 - mine) * half, half), half), :] = other_ref[...]


def mlp_kernel(
    tokens_ref, own_ref, other_ref, gain_ref, wg_ref, wu_ref, wd_ref,
    residual_ref, keep_ref, send_ref,
    part,
):
    joined(own_ref, other_ref, part)
    residual = tokens_ref[...].astype(F32) + part[...].astype(F32)
    residual_ref[...] = residual
    mean = jnp.mean(residual * residual, axis=-1, keepdims=True)
    second = (residual * lax.rsqrt(mean + EPSILON) * gain_ref[...]).astype(BF16)
    gate = dot_nn(second, wg_ref[...])
    up = dot_nn(second, wu_ref[...])
    hidden = (gate / (1.0 + jnp.exp(-gate)) * up).astype(BF16)
    part[...] = dot_nn(hidden, wd_ref[...]).astype(BF16)
    half = own_ref.shape[0]
    mine = lax.rem(lax.axis_index("tp"), 2)
    keep_ref[...] = part[pl.ds(pl.multiple_of(mine * half, half), half), :]
    send_ref[...] = part[pl.ds(pl.multiple_of((1 - mine) * half, half), half), :]


def close_kernel(residual_ref, own_ref, other_ref, out_ref, part):
    joined(own_ref, other_ref, part)
    out_ref[...] = (residual_ref[...] + part[...].astype(F32)).astype(BF16)


def settle_kernel(heads, shape, pair_cap, plan, *rest):
    nz, ny = shape
    count = nz * ny
    lanes = count * pair_cap
    inputs = rest[: len(plan)]
    state_ref, norm_ref, edge_ref, stage, flat, shifted, table, in_sem, out_sem = rest[len(plan) :]
    body = heads * LINES
    here = lax.axis_index("req")
    row_here, column_here = here // ny, here % ny
    loads = []
    for i, parts in enumerate(plan):
        for place, (dz, dy, first, size) in enumerate(parts):
            source = lax.rem(row_here - dz + nz, nz) * ny + lax.rem(column_here - dy + ny, ny)
            at = sum(p[3] for p in parts[:place])
            loads.append(
                pltpu.make_async_copy(
                    inputs[i].at[pl.ds(at, size)],
                    stage.at[pl.ds(source * pair_cap + first, size)],
                    in_sem.at[len(loads)],
                )
            )
    for load in loads:
        load.start()
    norm_ref[...] = jnp.zeros(norm_ref.shape, F32)
    edge_ref[...] = jnp.zeros(edge_ref.shape, BF16)
    for load in loads:
        load.wait()
    one_row = lax.broadcasted_iota(jnp.int32, (EXTRA, 128), 0)
    one_line = lax.broadcasted_iota(jnp.int32, (EXTRA, 128), 1)
    mark = (one_row == EXTRA - 1) & (one_line == 127)
    filled = jnp.int32(0)
    for lane in range(lanes):
        block = jnp.where(mark, stage[lane, body : body + EXTRA, :].astype(F32), 0.0)
        live = jnp.sum(block).astype(jnp.int32)
        table[filled] = lane
        filled = filled + live

    total = state_ref.shape[0]
    width = edge_ref.shape[2]
    edge_lines = -(-width // 128)
    lane_ids = lax.broadcasted_iota(jnp.int32, (LINES, 128), 1)
    head_ids = lax.broadcasted_iota(jnp.int32, (8, 128), 1)
    head_rows = lax.broadcasted_iota(jnp.int32, (8, 128), 0)
    stores = []
    done = 0
    for s in range(CAP):
        first, shift = line_of(s)
        last = -(-((s + 1) * SPAN) // 128)
        span = last - first

        @pl.when(s < filled)
        def _():
            lane = table[s]
            extra = stage[lane, body : body + EXTRA, :].astype(F32)
            pairs = [[], []]
            for j in range(2):
                for c in range(edge_lines):
                    end = min(width, 128 * (c + 1))
                    line = 2 * heads + edge_lines * j + c
                    pairs[j].append(extra[line : line + 1, : end - 128 * c])
            edge_ref[s] = jnp.concatenate(
                [jnp.concatenate(pairs[j], axis=1) for j in range(2)], axis=0
            ).astype(BF16)
            for h in range(heads):
                rows = stage[lane, h * LINES : (h + 1) * LINES, :].astype(F32)
                norm_ref[h, s : s + 1, :] = jnp.concatenate(
                    [
                        extra[2 * h : 2 * h + 1, :],
                        extra[2 * h + 1 : 2 * h + 2, :],
                        rows[LINES - 1 : LINES, : F - 256],
                    ],
                    axis=1,
                )
                if shift:
                    shifted[h, 8 : 8 + LINES, :] = rows
                    before = shifted[h, 7 : 7 + LINES, :]
                    rows = pltpu.roll(jnp.where(lane_ids < 128 - shift, rows, before), shift, 1)
                    old = flat[h, first : first + 1, :]
                    flat[h, first + 1 : last, :] = rows[1:span]
                    flat[h, first : first + 1, :] = jnp.where(head_ids[:1] < shift, old, rows[:1])
                else:
                    flat[h, first:last, :] = rows[:span]

        @pl.when(s >= filled)
        def _():
            for h in range(heads):
                if shift:
                    old = flat[h, first : first + 1, :]
                    flat[h, first + 1 : last, :] = jnp.zeros((span - 1, 128), F32)
                    flat[h, first : first + 1, :] = jnp.where(head_ids[:1] < shift, old, 0.0)
                else:
                    flat[h, first:last, :] = jnp.zeros((span, 128), F32)

        until = total if s == CAP - 1 else ((s + 1) * SPAN // 128) // 8 * 8
        for h in range(heads):
            store = pltpu.make_async_copy(
                flat.at[h, pl.ds(done, until - done)],
                state_ref.at[pl.ds(done, until - done), h],
                out_sem.at[s, h],
            )
            store.start()
            stores.append(store)
        done = until
    for store in stores:
        store.wait()


def shards(
    tokens, conv_edge, state_start, norm_start, accepted, owner, attn_gain, conv_weight,
    w_query, w_key, w_value, w_out, mlp_gain, w_gate, w_up, w_down,
):
    requests, steps, width = tokens.shape
    count = lax.axis_size("req")
    tp_size = lax.axis_size("tp")
    nz, ny = shape = grid_of(count)
    pair_cap = (CAP + count - 1) // count
    heads = w_query.shape[1] // FD
    rows_all = requests * steps
    lines = state_start.shape[1] // 128
    payload = heads * LINES + EXTRA
    column_width = width // tp_size
    line_pick, line_bias, plain_pick, plain_bias, phase_mask, turn = (jnp.asarray(t) for t in tables())

    vmem = pl.BlockSpec(memory_space=pltpu.VMEM)
    smem = pl.BlockSpec(memory_space=pltpu.SMEM)
    anywhere = pl.BlockSpec(memory_space=pl.ANY)
    limit = pltpu.CompilerParams(vmem_limit_bytes=48 * 2**20)

    flat_tokens = tokens.reshape(rows_all, width)
    lined_state = jnp.swapaxes(state_start.reshape(heads, lines, 128), 0, 1)
    piece_shape = jax.ShapeDtypeStruct((pair_cap, payload, 128), BF16)
    outs = pl.pallas_call(
        functools.partial(pack_kernel, heads, shape, pair_cap, tp_size),
        out_shape=[piece_shape] * count
        + [
            jax.ShapeDtypeStruct((rows_all, heads * FD), BF16),
            jax.ShapeDtypeStruct((rows_all, heads * FD), BF16),
            jax.ShapeDtypeStruct((rows_all, heads * DV), BF16),
            jax.ShapeDtypeStruct((requests, heads, LINES, 128), BF16),
        ],
        in_specs=[smem, smem, anywhere] + [vmem] * 14,
        out_specs=[anywhere] * count + [vmem] * 4,
        scratch_shapes=[
            pltpu.VMEM((heads, (lines + 1) // 8 * 8 + 8, 128), F32),
            pltpu.VMEM((requests * 24, width), F32),
            pltpu.VMEM((rows_all, width), BF16),
            pltpu.VMEM((heads, rows_all, 2 * WIDE), F32),
            pltpu.VMEM((heads, rows_all, 384), F32),
            pltpu.VMEM((heads, rows_all, PHASES * 128), BF16),
            pltpu.VMEM((2 * requests, -(-column_width // 128) * 128), F32),
            pltpu.VMEM((EXTRA, 128), F32),
            pltpu.VMEM((count * pair_cap, payload, 128), BF16),
            pltpu.SemaphoreType.DMA((heads,)),
            pltpu.SemaphoreType.DMA((count,)),
        ],
        compiler_params=limit,
        name="pack",
    )(
        owner, accepted, lined_state, flat_tokens, conv_edge, norm_start, attn_gain[None, :], conv_weight,
        w_query.T, w_key.T, w_value, line_pick, line_bias, plain_pick, plain_bias, phase_mask, turn,
    )
    pieces, (queries, keys, values, start_rows) = outs[:count], outs[count:]

    def moved(x, dz, dy):
        route = [
            (z * ny + y, (z + dz) % nz * ny + (y + dy) % ny) for z in range(nz) for y in range(ny)
        ]
        return lax.ppermute(x, "req", route)

    arrived, plan = [pieces[0]], [((0, 0, 0, pair_cap),)]
    for dz in range(nz):
        for dy in range(ny):
            if dz or dy:
                arrived.append(moved(pieces[dz * ny + dy], dz, dy))
                plan.append(((dz, dy, 0, pair_cap),))

    half_shape = jax.ShapeDtypeStruct((rows_all // 2, width), BF16)

    def summed(keep, send):
        swap = [(i, i ^ 1) for i in range(tp_size)]
        total = keep.astype(F32) + lax.ppermute(send, "tp", swap).astype(F32)
        step = 2
        while step < tp_size:
            rounded = total.astype(BF16)
            across = lax.ppermute(rounded, "tp", [(i, i ^ step) for i in range(tp_size)])
            total = rounded.astype(F32) + across.astype(F32)
            step *= 2
        rounded = total.astype(BF16)
        return rounded, lax.ppermute(rounded, "tp", swap)

    keep, send = pl.pallas_call(
        functools.partial(attend_kernel, heads, 0),
        out_shape=[half_shape] * 2,
        in_specs=[vmem] * 11,
        out_specs=[vmem] * 2,
        scratch_shapes=[
            pltpu.VMEM((heads, rows_all, DV), BF16),
            pltpu.VMEM((rows_all, width), BF16),
        ],
        compiler_params=limit,
        name="attend",
    )(
        queries, keys, values, start_rows, norm_start, w_out,
        line_pick, line_bias, plain_pick, plain_bias, phase_mask,
    )
    own, other = summed(keep, send)
    residual, keep, send = pl.pallas_call(
        mlp_kernel,
        out_shape=[jax.ShapeDtypeStruct((rows_all, width), F32)] + [half_shape] * 2,
        in_specs=[vmem] * 7,
        out_specs=[vmem] * 3,
        scratch_shapes=[pltpu.VMEM((rows_all, width), BF16)],
        compiler_params=limit,
        name="mlp",
    )(flat_tokens, own, other, mlp_gain[None, :], w_gate, w_up, w_down)
    own, other = summed(keep, send)
    hidden_out = pl.pallas_call(
        close_kernel,
        out_shape=jax.ShapeDtypeStruct((rows_all, width), BF16),
        in_specs=[vmem] * 3,
        out_specs=vmem,
        scratch_shapes=[pltpu.VMEM((rows_all, width), BF16)],
        compiler_params=limit,
        name="close",
    )(residual, own, other)

    out_lines = CAP * SPAN // 128
    kept_state, kept_norm, kept_edge = pl.pallas_call(
        functools.partial(settle_kernel, heads, shape, pair_cap, tuple(plan)),
        out_shape=[
            jax.ShapeDtypeStruct((out_lines, heads, 128), F32),
            jax.ShapeDtypeStruct((heads, CAP, F), F32),
            jax.ShapeDtypeStruct((CAP, 2, column_width), BF16),
        ],
        in_specs=[anywhere] * len(arrived),
        out_specs=[anywhere, vmem, vmem],
        scratch_shapes=[
            pltpu.VMEM((count * pair_cap, payload, 128), BF16),
            pltpu.VMEM((heads, out_lines, 128), F32),
            pltpu.VMEM((heads, LINES + 16, 128), F32),
            pltpu.SMEM((count * pair_cap + 1,), jnp.int32),
            pltpu.SemaphoreType.DMA((sum(len(p) for p in plan),)),
            pltpu.SemaphoreType.DMA((CAP, heads)),
        ],
        compiler_params=limit,
        name="settle",
    )(*arrived)
    return (
        hidden_out.reshape(requests, steps, width),
        jnp.swapaxes(kept_state, 0, 1).reshape(heads, out_lines * 128),
        kept_norm,
        kept_edge,
    )


def solution(mesh):
    placed = (
        P("req", None, None),
        P("req", None, None),
        P("tp", "req"),
        P("tp", "req", None),
        P("req"),
        P("req"),
        P(),
        P(),
        P(None, "tp"),
        P(None, "tp"),
        P("tp", None),
        P("tp", None),
        P(),
        P(None, "tp"),
        P(None, "tp"),
        P("tp", None),
    )
    return jax.shard_map(
        shards,
        mesh=mesh,
        in_specs=placed,
        out_specs=(
            P("req", None, None),
            P("tp", "req"),
            P("tp", "req", None),
            P("req", None, "tp"),
        ),
        check_vma=False,
    )
```

```python
import functools
import math

import jax
import jax.numpy as jnp
import numpy as np
from jax import lax
from jax.experimental import pallas as pl
from jax.experimental.pallas import tpu as pltpu
from jax.sharding import PartitionSpec as P

FD = 16
DV = 112
F = 273
CAP = 16
EPSILON = 1e-05

SPAN = F * DV
LINES = 240
WIDE = 256
PHASES = 7
EXTRA = 16
BF16 = jnp.bfloat16
F32 = jnp.float32


def line_of(index):
    return (index * SPAN) // 128, (index * SPAN) % 128


@functools.lru_cache(None)
def tables():
    scale_two = 0.25 * math.sqrt(0.5)

    def feature(column, f, left, right, bias):
        if f == 0:
            bias[0, column] = bias[1, column] = bias[2, column] = 1.0
        elif f <= FD:
            left[f - 1, column] = 1.0
            bias[1, column] = 1.0
            bias[2, column] = 0.5
        elif f < F:
            left[(f - 1 - FD) // FD, column] = 1.0
            right[(f - 1 - FD) % FD, column] = 1.0
            bias[2, column] = scale_two

    def build(width, places):
        left, right = np.zeros((FD, width)), np.zeros((FD, width))
        bias = np.zeros((8, width), np.float32)
        for column, f in places:
            feature(column, f, left, right, bias)
        return np.concatenate([left, right], 1).astype(BF16), bias

    lined = [
        (part * WIDE + m, 8 * (m // PHASES) + m % PHASES + part)
        for part in range(2)
        for m in range(LINES)
    ]
    line_pick, line_bias = build(2 * WIDE, lined)
    plain_pick, plain_bias = build(384, [(f, f) for f in range(F)])
    phase_mask = np.zeros((8, WIDE))
    for k in range(PHASES):
        phase_mask[k, k::PHASES] = 1.0
    turn = np.zeros((DV, PHASES * 128))
    for k in range(PHASES):
        for lane in range(128):
            turn[(16 * k + lane) % DV, 128 * k + lane] = 1.0
    table = np.zeros((DV + FD, 1792))
    table[:DV, : PHASES * 128] = turn
    table[:8, PHASES * 128 : PHASES * 128 + WIDE] = phase_mask
    table[DV:] = np.concatenate([line_pick, plain_pick], 1)
    return table.astype(BF16), np.concatenate([line_bias, plain_bias], 1)


def dot_nt(a, b):
    return lax.dot_general(a, b, (((1,), (1,)), ((), ())), preferred_element_type=F32)


def dot_tn(a, b):
    return lax.dot_general(a, b, (((0,), (0,)), ((), ())), preferred_element_type=F32)


def dot_nn(a, b):
    return jnp.dot(a, b, preferred_element_type=F32)


def expand(x, table_ref, bias_ref, start, width):
    both = dot_nn(x, table_ref[DV:, 2 * start : 2 * (start + width)])
    bias = bias_ref[:, start : start + width]
    left = both[:, :width] + bias[0:1, :]
    right = both[:, width:] + bias[1:2, :]
    return left * right * bias[2:3, :]


def lined_phi(x, table_ref, bias_ref):
    return expand(x, table_ref, bias_ref, 0, 2 * WIDE)


def plain_phi(x, table_ref, bias_ref):
    return expand(x, table_ref, bias_ref, 2 * WIDE, 384)


def spread(phi, table_ref):
    pieces = []
    for k in range(PHASES):
        chosen = table_ref[k : k + 1, PHASES * 128 : PHASES * 128 + WIDE]
        for part in range(2):
            pieces.append(phi[:, part * WIDE : (part + 1) * WIDE] * chosen)
    return jnp.concatenate(pieces, axis=0)


def pack_kernel(
    heads, count, pair_cap, tp_size, loaded, made,
    state_ref, *rest,
):
    fetched, rest = rest[:loaded], rest[loaded:]
    pieces, rest = rest[:made], rest[made:]
    (q_ref, k_ref, v_ref, start_ref), rest = rest[:4], rest[4:]
    held, rest = rest[:loaded], rest[loaded:]
    flat, padded, mixed, phi, plain, turned, edges, extra, stage, begun, none, state_sem, load_sem, none_sem, out_sem, begun_sem = rest
    fetches = [pltpu.make_async_copy(fetched[i], held[i], load_sem.at[i]) for i in range(loaded)]
    for fetch in fetches:
        fetch.start()
    lines = state_ref.shape[0]
    loads = [
        pltpu.make_async_copy(state_ref.at[:, h], flat.at[h, pl.ds(0, lines)], state_sem.at[h])
        for h in range(heads)
    ]
    for load in loads:
        load.start()
    (
        owner_ref, accepted_ref, tokens_ref, edge_ref, gain_ref, conv_ref,
        wq_ref, wk_ref, wv_ref, table_ref, bias_ref, norm_ref,
    ) = held
    requests = owner_ref.shape[0]
    steps = tokens_ref.shape[0] // requests
    body = heads * LINES
    empty = [piece.at[i, pl.ds(body, EXTRA)] for piece in pieces for i in range(piece.shape[0])]
    blanks = [pltpu.make_async_copy(none, place, none_sem.at[i]) for i, place in enumerate(empty)]
    for fetch in fetches[:6]:
        fetch.wait()
    ranks, seconds, second = [], [], jnp.int32(0)
    for r in range(requests):
        rank = jnp.int32(0)
        for earlier in range(r):
            rank = rank + (owner_ref[earlier] == owner_ref[r]).astype(jnp.int32)
        ranks.append(rank)
        seconds.append((rank == 1) & (second == 0))
        second = second + (rank == 1).astype(jnp.int32)
    one_line = lax.broadcasted_iota(jnp.int32, (EXTRA, 128), 1)
    one_row = lax.broadcasted_iota(jnp.int32, (EXTRA, 128), 0)
    last = one_row == EXTRA - 1
    count_mark = jnp.where(last & (one_line == 126), second.astype(F32), 0.0)
    none[...] = count_mark.astype(BF16)
    for blank in blanks:
        blank.start()

    tp_here = lax.axis_index("tp")
    gain = gain_ref[...].reshape(1, gain_ref.shape[0])
    for r in range(requests):
        base = 24 * r
        wide = tokens_ref[steps * r : steps * (r + 1), :].astype(F32)
        mean = jnp.mean(wide * wide, axis=-1, keepdims=True)
        normed = (wide * lax.rsqrt(mean + EPSILON) * gain).astype(BF16).astype(F32)
        padded[base + 8 : base + 8 + steps, :] = normed
        padded[base : base + 8, :] = jnp.zeros((8, wide.shape[1]), F32)
        padded[base + 6 : base + 8, :] = edge_ref[r].astype(F32)
        convolved = conv_ref[2:3, :] * normed
        for tap in range(2):
            convolved = convolved + conv_ref[tap : tap + 1, :] * padded[base + 6 + tap : base + 6 + tap + steps, :]
        blend = normed + convolved / (1.0 + jnp.exp(-normed))
        mixed[steps * r : steps * (r + 1), :] = blend.astype(BF16)

    for fetch in fetches[6:]:
        fetch.wait()
    queries = dot_nt(mixed[...], wq_ref[...]).astype(BF16)
    keys = dot_nt(mixed[...], wk_ref[...]).astype(BF16)
    values = dot_nt(mixed[...], wv_ref[...]).astype(BF16)
    q_ref[...] = queries
    k_ref[...] = keys
    v_ref[...] = values

    for h in range(heads):
        key = keys[:, FD * h : FD * (h + 1)]
        phi[h] = lined_phi(key, table_ref, bias_ref)
        plain[h] = plain_phi(key, table_ref, bias_ref)
        turned[h] = dot_nn(values[:, DV * h : DV * (h + 1)], table_ref[:DV, : PHASES * 128]).astype(BF16)

    column_width = tokens_ref.shape[1] // tp_size
    edge_rows = lax.broadcasted_iota(jnp.int32, (2 * requests, 24 * requests), 0)
    edge_columns = lax.broadcasted_iota(jnp.int32, (2 * requests, 24 * requests), 1)
    wanted = jnp.zeros(edge_rows.shape, jnp.int32)
    for r in range(requests):
        wanted = jnp.where(edge_rows // 2 == r, 24 * r + 6 + accepted_ref[r] + edge_rows % 2, wanted)
    choose = (edge_columns == wanted).astype(F32).astype(BF16)
    for i in range(tp_size):
        @pl.when(tp_here == i)
        def _():
            window = padded[:, column_width * i : column_width * (i + 1)].astype(BF16)
            edges[:, :column_width] = dot_nn(choose, window)

    lane_ids = lax.broadcasted_iota(jnp.int32, (LINES, 128), 1)
    step_ids = lax.broadcasted_iota(jnp.int32, (steps, 1), 0)
    edge_lines = -(-column_width // 128)
    for load in loads:
        load.wait()
    for blank in blanks:
        blank.wait()
    sends, keeps = [], []
    for r in range(requests):
        owner = owner_ref[r]
        taken = (step_ids < accepted_ref[r]).astype(F32)
        first, shift = line_of(r)
        extra[...] = jnp.zeros((EXTRA, 128), F32)
        for h in range(heads):
            rows = slice(steps * r, steps * (r + 1))
            spread_keys = spread((phi[h, rows, :] * taken).astype(BF16), table_ref)
            value_rows = turned[h, rows, :]
            parts = []
            for k in range(PHASES):
                block = value_rows[:, 128 * k : 128 * (k + 1)]
                early = one_line < DV - 16 * k
                zero = jnp.zeros((steps, 128), BF16)
                parts.append(jnp.where(early, block, zero))
                parts.append(jnp.where(early, zero, block))
            added = dot_tn(spread_keys, jnp.concatenate(parts, axis=0))[:LINES]
            start = flat[h, first : first + LINES, :]
            if shift:
                following = flat[h, first + 1 : first + 1 + LINES, :]
                start = pltpu.roll(jnp.where(lane_ids >= shift, start, following), 128 - shift, 1)
            begun[r, h] = start.astype(BF16)
            kept = start + added
            sums = jnp.sum(plain[h, rows, :] * taken, axis=0, keepdims=True)[:, :F] + norm_ref[h, r : r + 1, :]
            extra[2 * h : 2 * h + 1, :] = sums[:, :128]
            extra[2 * h + 1 : 2 * h + 2, :] = sums[:, 128:256]
            tail = jnp.concatenate([sums[:, 256:], jnp.zeros((1, 128 - (F - 256)), F32)], axis=1)
            stage[r, h * LINES : (h + 1) * LINES - 16, :] = kept[: LINES - 16].astype(BF16)
            stage[r, (h + 1) * LINES - 16 : (h + 1) * LINES, :] = jnp.where(
                one_row == 15, tail, kept[LINES - 16 :]
            ).astype(BF16)
        for j in range(2):
            for c in range(edge_lines):
                end = min(column_width, 128 * (c + 1))
                line = 2 * heads + edge_lines * j + c
                extra[line : line + 1, : end - 128 * c] = edges[2 * r + j : 2 * r + j + 1, 128 * c : end]
        marked = jnp.where(last & (one_line == 127), (owner + 1).astype(F32), extra[...] + count_mark)
        stage[r, body : body + EXTRA, :] = marked.astype(BF16)
        keep = pltpu.make_async_copy(begun.at[r], start_ref.at[r], begun_sem.at[r])
        keep.start()
        keeps.append(keep)
        if pair_cap == 1:
            routes = [(ranks[r] == 0, pieces[0].at[owner])]
        else:
            far = owner ^ lax.axis_index("req")
            routes = [((ranks[r] == 0) & (far == k), pieces[k].at[0]) for k in range(count)]
            routes += [(seconds[r], pieces[k].at[1]) for k in range(5)]
            routes += [(ranks[r] == 1, pieces[count].at[owner])]
        for i, (chosen, place) in enumerate(routes):
            send = pltpu.make_async_copy(stage.at[r], place, out_sem.at[r, i])
            sends.append((chosen, send))

            @pl.when(chosen)
            def _():
                send.start()
    for chosen, send in sends:
        @pl.when(chosen)
        def _():
            send.wait()
    for keep in keeps:
        keep.wait()


def attend_kernel(
    heads,
    q_ref, k_ref, v_ref, start_ref, norm_ref, wo_ref, table_ref, bias_ref,
    part_ref,
    attended,
):
    requests = start_ref.shape[0]
    rows_all = q_ref.shape[0]
    steps = rows_all // requests
    row_ids = lax.broadcasted_iota(jnp.int32, (rows_all, rows_all), 0)
    column_ids = lax.broadcasted_iota(jnp.int32, (rows_all, rows_all), 1)
    allowed = (row_ids // steps == column_ids // steps) & (row_ids >= column_ids)
    lane_ids = lax.broadcasted_iota(jnp.int32, (steps, 128), 1)
    for h in range(heads):
        query = q_ref[:, FD * h : FD * (h + 1)]
        key = k_ref[:, FD * h : FD * (h + 1)]
        value = v_ref[:, DV * h : DV * (h + 1)]
        phi = lined_phi(query, table_ref, bias_ref).astype(BF16)
        plain = plain_phi(query, table_ref, bias_ref)
        inner = dot_nt(query, key) * 0.25
        scores = jnp.where(allowed, 1.0 + inner + 0.5 * inner * inner, 0.0)
        below = jnp.sum(scores, axis=-1, keepdims=True)
        within = dot_nn(scores.astype(BF16), value)
        for r in range(requests):
            rows = slice(steps * r, steps * (r + 1))
            spread_query = spread(phi[rows], table_ref)[:, :LINES]
            lined = dot_nn(spread_query, start_ref[r, h])
            total = jnp.zeros((steps, 128), F32)
            for j in range(PHASES + 1):
                block = jnp.zeros((steps, 128), F32)
                if j < PHASES:
                    at = steps * (2 * j)
                    block = jnp.where(lane_ids < DV - 16 * j, lined[at : at + steps], 0.0)
                if j > 0:
                    at = steps * (2 * (j - 1) + 1)
                    block = jnp.where(lane_ids >= DV - 16 * (j - 1), lined[at : at + steps], block)
                total = total + (pltpu.roll(block, 16 * j, 1) if 0 < j < 8 else block)
            beneath = below[rows] + jnp.sum(plain[rows, :F] * norm_ref[h, r : r + 1, :], axis=-1, keepdims=True)
            attended[h, rows, :] = ((total[:, :DV] + within[rows]) / beneath).astype(BF16)
    out = dot_nn(attended[0], wo_ref[0:DV, :])
    for h in range(1, heads):
        out = out + dot_nn(attended[h], wo_ref[DV * h : DV * (h + 1), :])
    part_ref[...] = out.astype(BF16)


def mlp_kernel(tokens_ref, sum_ref, gain_ref, wg_ref, wu_ref, wd_ref, residual_ref, part_ref):
    residual = tokens_ref[...].astype(F32) + sum_ref[...].astype(F32)
    residual_ref[...] = residual
    mean = jnp.mean(residual * residual, axis=-1, keepdims=True)
    gain = gain_ref[...].reshape(1, gain_ref.shape[0])
    second = (residual * lax.rsqrt(mean + EPSILON) * gain).astype(BF16)
    gate = dot_nn(second, wg_ref[...])
    up = dot_nn(second, wu_ref[...])
    hidden = (gate / (1.0 + jnp.exp(-gate)) * up).astype(BF16)
    part_ref[...] = dot_nn(hidden, wd_ref[...]).astype(BF16)


def close_kernel(residual_ref, sum_ref, *rest):
    marks, (out_ref, several_ref, lines, sems) = rest[:-4], rest[-4:]
    reads = [
        pltpu.make_async_copy(mark.at[0, pl.ds(mark.shape[1] - EXTRA, EXTRA)], lines.at[i], sems.at[i])
        for i, mark in enumerate(marks)
    ]
    for read in reads:
        read.start()
    out_ref[...] = (residual_ref[...] + sum_ref[...].astype(F32)).astype(BF16)
    for read in reads:
        read.wait()
    several_ref[0] = jnp.int32(0)
    if marks:
        row = lax.broadcasted_iota(jnp.int32, (EXTRA, 128), 0)
        lane = lax.broadcasted_iota(jnp.int32, (EXTRA, 128), 1)
        most = functools.reduce(jnp.maximum, [lines[i].astype(F32) for i in range(len(marks))])
        most = jnp.max(jnp.where((row == EXTRA - 1) & (lane == 126), most, 0.0))
        several_ref[0] = (most > 1.0).astype(jnp.int32)


def settle_kernel(heads, count, pair_cap, direct, arrivals, *rest):
    lanes = count * pair_cap
    body = heads * LINES
    here = lax.axis_index("req")
    inputs, rest = rest[:arrivals], rest[arrivals:]
    state_ref, norm_ref, edge_ref, stage, flat, shifted, table, in_sem, out_sem = rest
    loads = []

    def load(place, lane):
        loads.append(pltpu.make_async_copy(place, stage.at[lane], in_sem.at[len(loads)]))

    for i in range(count):
        if pair_cap == 1:
            load(inputs[0].at[i], i)
        else:
            source = here ^ i
            load(inputs[i].at[0], 2 * source)
            if direct:
                load(inputs[i].at[1] if i < 5 else inputs[count + i - 5].at[0], 2 * source + 1)
            else:
                load(inputs[count].at[i], 2 * i + 1)
    for copy in loads:
        copy.start()
    norm_ref[...] = jnp.zeros(norm_ref.shape, F32)
    edge_ref[...] = jnp.zeros(edge_ref.shape, BF16)
    for copy in loads:
        copy.wait()
    one_row = lax.broadcasted_iota(jnp.int32, (EXTRA, 128), 0)
    one_line = lax.broadcasted_iota(jnp.int32, (EXTRA, 128), 1)
    mark = (one_row == EXTRA - 1) & (one_line == 127)
    filled = jnp.int32(0)
    for lane in range(lanes):
        block = jnp.where(mark, stage[lane, body : body + EXTRA, :].astype(F32), 0.0)
        live = jnp.sum(block).astype(jnp.int32) == here + 1
        table[filled] = lane
        filled = filled + live.astype(jnp.int32)

    total = state_ref.shape[0]
    width = edge_ref.shape[2]
    edge_lines = -(-width // 128)
    lane_ids = lax.broadcasted_iota(jnp.int32, (LINES, 128), 1)
    head_ids = lax.broadcasted_iota(jnp.int32, (8, 128), 1)
    head_rows = lax.broadcasted_iota(jnp.int32, (8, 128), 0)
    stores = []
    done = 0
    for s in range(CAP):
        first, shift = line_of(s)
        last = -(-((s + 1) * SPAN) // 128)
        span = last - first

        @pl.when(s < filled)
        def _():
            lane = table[s]
            extra = stage[lane, body : body + EXTRA, :].astype(F32)
            pairs = [[], []]
            for j in range(2):
                for c in range(edge_lines):
                    end = min(width, 128 * (c + 1))
                    line = 2 * heads + edge_lines * j + c
                    pairs[j].append(extra[line : line + 1, : end - 128 * c])
            edge_ref[s] = jnp.concatenate(
                [jnp.concatenate(pairs[j], axis=1) for j in range(2)], axis=0
            ).astype(BF16)
            for h in range(heads):
                rows = stage[lane, h * LINES : (h + 1) * LINES, :].astype(F32)
                norm_ref[h, s : s + 1, :] = jnp.concatenate(
                    [
                        extra[2 * h : 2 * h + 1, :],
                        extra[2 * h + 1 : 2 * h + 2, :],
                        rows[LINES - 1 : LINES, : F - 256],
                    ],
                    axis=1,
                )
                if shift:
                    shifted[h, 8 : 8 + LINES, :] = rows
                    before = shifted[h, 7 : 7 + LINES, :]
                    rows = pltpu.roll(jnp.where(lane_ids < 128 - shift, rows, before), shift, 1)
                    old = flat[h, first : first + 1, :]
                    flat[h, first + 1 : last, :] = rows[1:span]
                    flat[h, first : first + 1, :] = jnp.where(head_ids[:1] < shift, old, rows[:1])
                else:
                    flat[h, first:last, :] = rows[:span]

        @pl.when(s >= filled)
        def _():
            for h in range(heads):
                if shift:
                    old = flat[h, first : first + 1, :]
                    flat[h, first + 1 : last, :] = jnp.zeros((span - 1, 128), F32)
                    flat[h, first : first + 1, :] = jnp.where(head_ids[:1] < shift, old, 0.0)
                else:
                    flat[h, first:last, :] = jnp.zeros((span, 128), F32)

        until = total if s == CAP - 1 else ((s + 1) * SPAN // 128) // 8 * 8
        for h in range(heads):
            store = pltpu.make_async_copy(
                flat.at[h, pl.ds(done, until - done)],
                state_ref.at[pl.ds(done, until - done), h],
                out_sem.at[s, h],
            )
            store.start()
            stores.append(store)
        done = until
    for store in stores:
        store.wait()


def shards(
    tokens, conv_edge, state_start, norm_start, accepted, owner, attn_gain, conv_weight,
    w_query, w_key, w_value, w_out, mlp_gain, w_gate, w_up, w_down,
):
    requests, steps, width = tokens.shape
    count = lax.axis_size("req")
    tp_size = lax.axis_size("tp")
    pair_cap = (CAP + count - 1) // count
    heads = w_query.shape[1] // FD
    rows_all = requests * steps
    lines = state_start.shape[1] // 128
    payload = heads * LINES + EXTRA
    column_width = width // tp_size
    table, bias = (jnp.asarray(t) for t in tables())

    vmem = pl.BlockSpec(memory_space=pltpu.VMEM)
    smem = pl.BlockSpec(memory_space=pltpu.SMEM)
    hbm = pl.BlockSpec(memory_space=pltpu.HBM)
    anywhere = pl.BlockSpec(memory_space=pl.ANY)
    limit = functools.partial(pltpu.CompilerParams, vmem_limit_bytes=40 * 2**20)

    def cost(us):
        return pl.CostEstimate(flops=0, transcendentals=0, bytes_accessed=int(us * 3.6e2))

    flat_tokens = tokens.reshape(rows_all, width)
    lined_state = jnp.swapaxes(state_start.reshape(heads, lines, 128), 0, 1)
    held = [count] if pair_cap == 1 else [2] * 5 + [1] * 3 + [count]
    piece_shapes = [jax.ShapeDtypeStruct((size, payload, 128), BF16) for size in held]
    fetched = [
        owner, accepted, flat_tokens, conv_edge, attn_gain, conv_weight,
        w_query.T, w_key.T, w_value, table, bias, norm_start,
    ]
    outs = pl.pallas_call(
        functools.partial(pack_kernel, heads, count, pair_cap, tp_size, len(fetched), len(held)),
        out_shape=piece_shapes
        + [
            jax.ShapeDtypeStruct((rows_all, heads * FD), BF16),
            jax.ShapeDtypeStruct((rows_all, heads * FD), BF16),
            jax.ShapeDtypeStruct((rows_all, heads * DV), BF16),
            jax.ShapeDtypeStruct((requests, heads, LINES, 128), BF16),
        ],
        in_specs=[hbm] * (1 + len(fetched)),
        out_specs=[anywhere] * len(held) + [vmem] * 3 + [anywhere],
        scratch_shapes=[pltpu.SMEM(x.shape, x.dtype) for x in fetched[:2]]
        + [pltpu.VMEM(x.shape, x.dtype) for x in fetched[2:]]
        + [
            pltpu.VMEM((heads, (lines + 1) // 8 * 8 + 8, 128), F32),
            pltpu.VMEM((requests * 24, width), F32),
            pltpu.VMEM((rows_all, width), BF16),
            pltpu.VMEM((heads, rows_all, 2 * WIDE), F32),
            pltpu.VMEM((heads, rows_all, 384), F32),
            pltpu.VMEM((heads, rows_all, PHASES * 128), BF16),
            pltpu.VMEM((2 * requests, -(-column_width // 128) * 128), F32),
            pltpu.VMEM((EXTRA, 128), F32),
            pltpu.VMEM((requests, payload, 128), BF16),
            pltpu.VMEM((requests, heads, LINES, 128), BF16),
            pltpu.VMEM((EXTRA, 128), BF16),
            pltpu.SemaphoreType.DMA((heads,)),
            pltpu.SemaphoreType.DMA((len(fetched),)),
            pltpu.SemaphoreType.DMA((sum(held),)),
            pltpu.SemaphoreType.DMA((requests, count + 6)),
            pltpu.SemaphoreType.DMA((requests,)),
        ],
        compiler_params=limit(vmem_limit_bytes=60 * 2**20),
        cost_estimate=cost(8),
        name="pack",
    )(lined_state, *fetched)
    pieces, (queries, keys, values, start_rows) = list(outs[: len(held)]), outs[len(held) :]

    def swapped(x, far):
        return lax.ppermute(x, "req", [(i, i ^ far) for i in range(count)])

    arrived = {}

    def wave(now, fars, waits, later):
        for far in fars:
            arrived[far] = swapped(pieces[far], far)
        now, done, held_back = lax.optimization_barrier(
            (now, [arrived[far] for far in waits], [pieces[far] for far in later])
        )
        for far, x in zip(waits, done):
            arrived[far] = x
        for far, x in zip(later, held_back):
            pieces[far] = x
        return now

    cores = [[i, i + 1] for i in range(0, tp_size, 2)]
    chips = [list(range(core, tp_size, 2)) for core in range(2)]

    def summed(part, meet=lambda x: x):
        half = rows_all // 2
        both = lax.all_gather(part, "tp", axis=0, axis_index_groups=cores)
        mine = lax.dynamic_slice_in_dim(both, lax.axis_index("tp") % 2 * half, half, 1)
        mine = meet(jnp.sum(mine.astype(F32), axis=0).astype(BF16))
        mine = lax.all_gather(mine, "tp", axis=0, axis_index_groups=chips)
        mine = jnp.sum(mine.astype(F32), axis=0).astype(BF16)
        return lax.all_gather(mine, "tp", axis=0, tiled=True, axis_index_groups=cores)

    part = pl.pallas_call(
        functools.partial(attend_kernel, heads),
        out_shape=jax.ShapeDtypeStruct((rows_all, width), BF16),
        in_specs=[vmem] * 8,
        out_specs=vmem,
        scratch_shapes=[pltpu.VMEM((heads, rows_all, DV), BF16)],
        compiler_params=limit(),
        cost_estimate=cost(3),
        name="attend",
    )(
        queries, keys, values, start_rows, norm_start, w_out, table, bias,
    )
    total = summed(part)
    residual, part = pl.pallas_call(
        mlp_kernel,
        out_shape=[jax.ShapeDtypeStruct((rows_all, width), F32), jax.ShapeDtypeStruct((rows_all, width), BF16)],
        in_specs=[vmem] * 6,
        out_specs=[vmem] * 2,
        compiler_params=limit(),
        cost_estimate=cost(3),
        name="mlp",
    )(flat_tokens, total, mlp_gain, w_gate, w_up, w_down)
    forward = {}

    def half_way(x):
        if pair_cap > 1:
            x = wave(x, (4, 5, 2, 1, 3), (4, 5, 2, 1, 3), (6, 7))
            passed = arrived[4][1:2]
            forward.update({far: swapped(passed, far) for far in (1, 2, 3)})
        return x

    total = summed(part, half_way)
    if pair_cap > 1:
        total, forward = wave((total, forward), (6, 7), (6, 7), ())
    firsts, items = [], []
    if pair_cap > 1:
        arrived[0] = pieces[0]
        firsts = [arrived[far] for far in range(count)]
        items = [forward[far] for far in (1, 2, 3)]
    hidden_out, several = pl.pallas_call(
        close_kernel,
        out_shape=[jax.ShapeDtypeStruct((rows_all, width), BF16), jax.ShapeDtypeStruct((1,), jnp.int32)],
        in_specs=[vmem] * 2 + [anywhere] * len(firsts),
        out_specs=[vmem, smem],
        scratch_shapes=[pltpu.VMEM((count, EXTRA, 128), BF16), pltpu.SemaphoreType.DMA((count,))],
        compiler_params=limit(),
        cost_estimate=cost(1),
        name="close",
    )(residual, total, *firsts)

    out_lines = CAP * SPAN // 128

    def settled(direct, *inputs):
        return pl.pallas_call(
            functools.partial(settle_kernel, heads, count, pair_cap, direct, len(inputs)),
            out_shape=[
                jax.ShapeDtypeStruct((out_lines, heads, 128), F32),
                jax.ShapeDtypeStruct((heads, CAP, F), F32),
                jax.ShapeDtypeStruct((CAP, 2, column_width), BF16),
            ],
            in_specs=[anywhere] * len(inputs),
            out_specs=[anywhere, vmem, vmem],
            scratch_shapes=[
                pltpu.VMEM((count * pair_cap, payload, 128), BF16),
                pltpu.VMEM((heads, out_lines, 128), F32),
                pltpu.VMEM((heads, LINES + 16, 128), F32),
                pltpu.SMEM((count * pair_cap + 1,), jnp.int32),
                pltpu.SemaphoreType.DMA((count * pair_cap,)),
                pltpu.SemaphoreType.DMA((CAP, heads)),
            ],
            compiler_params=limit(),
            cost_estimate=cost(7),
            name="settle" if direct else "settle_general",
        )(*inputs)

    def exchanged(x):
        return lax.all_to_all(x, "req", 0, 0, tiled=True)

    if pair_cap > 1:
        kept_state, kept_norm, kept_edge = lax.cond(
            several[0] > 0,
            lambda firsts, items, spare: settled(False, *firsts, exchanged(spare)),
            lambda firsts, items, spare: settled(True, *firsts, *items),
            firsts, items, pieces[count],
        )
    else:
        kept_state, kept_norm, kept_edge = settled(True, exchanged(pieces[0]))
    return (
        hidden_out.reshape(requests, steps, width),
        jnp.swapaxes(kept_state, 0, 1).reshape(heads, out_lines * 128),
        kept_norm,
        kept_edge,
    )


def solution(mesh):
    placed = (
        P("req", None, None),
        P("req", None, None),
        P("tp", "req"),
        P("tp", "req", None),
        P("req"),
        P("req"),
        P(),
        P(),
        P(None, "tp"),
        P(None, "tp"),
        P("tp", None),
        P("tp", None),
        P(),
        P(None, "tp"),
        P(None, "tp"),
        P("tp", None),
    )
    return jax.shard_map(
        shards,
        mesh=mesh,
        in_specs=placed,
        out_specs=(
            P("req", None, None),
            P("tp", "req"),
            P("tp", "req", None),
            P("req", None, "tp"),
        ),
        check_vma=False,
    )
```

```python
import functools
import math

import jax
import jax.numpy as jnp
import numpy as np
from jax import lax
from jax.experimental import pallas as pl
from jax.experimental.pallas import tpu as pltpu
from jax.sharding import PartitionSpec as P

FD = 16
DV = 112
F = 273
CAP = 16
EPSILON = 1e-05

SPAN = F * DV
LINES = 240
WIDE = 256
PHASES = 7
EXTRA = 16
BF16 = jnp.bfloat16
F32 = jnp.float32


def line_of(index):
    return (index * SPAN) // 128, (index * SPAN) % 128


@functools.lru_cache(None)
def tables():
    scale_two = 0.25 * math.sqrt(0.5)

    def feature(column, f, left, right, bias):
        if f == 0:
            bias[0, column] = bias[1, column] = bias[2, column] = 1.0
        elif f <= FD:
            left[f - 1, column] = 1.0
            bias[1, column] = 1.0
            bias[2, column] = 0.5
        elif f < F:
            left[(f - 1 - FD) // FD, column] = 1.0
            right[(f - 1 - FD) % FD, column] = 1.0
            bias[2, column] = scale_two

    def build(width, places):
        left, right = np.zeros((FD, width)), np.zeros((FD, width))
        bias = np.zeros((8, width), np.float32)
        for column, f in places:
            feature(column, f, left, right, bias)
        return np.concatenate([left, right], 1).astype(BF16), bias

    lined = [
        (part * WIDE + m, 8 * (m // PHASES) + m % PHASES + part)
        for part in range(2)
        for m in range(LINES)
    ]
    line_pick, line_bias = build(2 * WIDE, lined)
    plain_pick, plain_bias = build(384, [(f, f) for f in range(F)])
    phase_mask = np.zeros((8, WIDE))
    for k in range(PHASES):
        phase_mask[k, k::PHASES] = 1.0
    turn = np.zeros((DV, PHASES * 128))
    for k in range(PHASES):
        for lane in range(128):
            turn[(16 * k + lane) % DV, 128 * k + lane] = 1.0
    table = np.zeros((DV + FD, 1792))
    table[:DV, : PHASES * 128] = turn
    table[:8, PHASES * 128 : PHASES * 128 + WIDE] = phase_mask
    table[DV:] = np.concatenate([line_pick, plain_pick], 1)
    return table.astype(BF16), np.concatenate([line_bias, plain_bias], 1)


def dot_nt(a, b):
    return lax.dot_general(a, b, (((1,), (1,)), ((), ())), preferred_element_type=F32)


def dot_tn(a, b):
    return lax.dot_general(a, b, (((0,), (0,)), ((), ())), preferred_element_type=F32)


def dot_nn(a, b):
    return jnp.dot(a, b, preferred_element_type=F32)


def expand(x, table_ref, bias_ref, start, width):
    both = dot_nn(x, table_ref[DV:, 2 * start : 2 * (start + width)])
    bias = bias_ref[:, start : start + width]
    left = both[:, :width] + bias[0:1, :]
    right = both[:, width:] + bias[1:2, :]
    return left * right * bias[2:3, :]


def lined_phi(x, table_ref, bias_ref):
    return expand(x, table_ref, bias_ref, 0, 2 * WIDE)


def plain_phi(x, table_ref, bias_ref):
    return expand(x, table_ref, bias_ref, 2 * WIDE, 384)


def spread(phi, table_ref):
    pieces = []
    for k in range(PHASES):
        chosen = table_ref[k : k + 1, PHASES * 128 : PHASES * 128 + WIDE]
        for part in range(2):
            pieces.append(phi[:, part * WIDE : (part + 1) * WIDE] * chosen)
    return jnp.concatenate(pieces, axis=0)


def pack_kernel(
    heads, count, pair_cap, tp_size, loaded, made,
    state_ref, *rest,
):
    fetched, rest = rest[:loaded], rest[loaded:]
    pieces, rest = rest[:made], rest[made:]
    (q_ref, k_ref, v_ref, start_ref), rest = rest[:4], rest[4:]
    held, rest = rest[:loaded], rest[loaded:]
    flat, padded, mixed, phi, plain, turned, edges, extra, stage, begun, kept_q, kept_k, kept_v, none, state_sem, load_sem, none_sem, out_sem, begun_sem = rest
    fetches = [pltpu.make_async_copy(fetched[i], held[i], load_sem.at[i]) for i in range(loaded)]
    for fetch in fetches:
        fetch.start()
    (
        owner_ref, accepted_ref, tokens_ref, edge_ref, gain_ref, conv_ref,
        wq_ref, wk_ref, wv_ref, table_ref, bias_ref, norm_ref,
    ) = held
    requests = owner_ref.shape[0]
    steps = tokens_ref.shape[0] // requests
    body = heads * LINES
    empty = [piece.at[i, pl.ds(body, EXTRA)] for piece in pieces for i in range(piece.shape[0])]
    blanks = [pltpu.make_async_copy(none, place, none_sem.at[i]) for i, place in enumerate(empty)]
    for fetch in fetches[:6]:
        fetch.wait()
    ranks, seconds, second = [], [], jnp.int32(0)
    for r in range(requests):
        rank = jnp.int32(0)
        for earlier in range(r):
            rank = rank + (owner_ref[earlier] == owner_ref[r]).astype(jnp.int32)
        ranks.append(rank)
        seconds.append((rank == 1) & (second == 0))
        second = second + (rank == 1).astype(jnp.int32)
    one_line = lax.broadcasted_iota(jnp.int32, (EXTRA, 128), 1)
    one_row = lax.broadcasted_iota(jnp.int32, (EXTRA, 128), 0)
    last = one_row == EXTRA - 1
    count_mark = jnp.where(last & (one_line == 126), second.astype(F32), 0.0)
    none[...] = count_mark.astype(BF16)
    for blank in blanks:
        blank.start()

    tp_here = lax.axis_index("tp")
    gain = gain_ref[...].reshape(1, gain_ref.shape[0])
    for r in range(requests):
        base = 24 * r
        wide = tokens_ref[steps * r : steps * (r + 1), :].astype(F32)
        mean = jnp.mean(wide * wide, axis=-1, keepdims=True)
        normed = (wide * lax.rsqrt(mean + EPSILON) * gain).astype(BF16).astype(F32)
        padded[base + 8 : base + 8 + steps, :] = normed
        padded[base : base + 8, :] = jnp.zeros((8, wide.shape[1]), F32)
        padded[base + 6 : base + 8, :] = edge_ref[r].astype(F32)
        convolved = conv_ref[2:3, :] * normed
        for tap in range(2):
            convolved = convolved + conv_ref[tap : tap + 1, :] * padded[base + 6 + tap : base + 6 + tap + steps, :]
        blend = normed + convolved / (1.0 + jnp.exp(-normed))
        mixed[steps * r : steps * (r + 1), :] = blend.astype(BF16)

    lines = state_ref.shape[0]
    cuts = [0] + [-(-(line_of(r)[0] + 3) // 8) * 8 for r in range(2, requests, 2)] + [lines]
    loads = [
        [
            pltpu.make_async_copy(
                state_ref.at[pl.ds(begin, end - begin), h], flat.at[h, pl.ds(begin, end - begin)], state_sem.at[i, h]
            )
            for h in range(heads)
        ]
        for i, (begin, end) in enumerate(zip(cuts, cuts[1:]))
    ]
    for part in loads:
        for load in part:
            load.start()
    for fetch in fetches[6:]:
        fetch.wait()
    queries = dot_nt(mixed[...], wq_ref[...]).astype(BF16)
    keys = dot_nt(mixed[...], wk_ref[...]).astype(BF16)
    values = dot_nt(mixed[...], wv_ref[...]).astype(BF16)
    keeps = []
    for i, (place, rows, x) in enumerate(
        ((q_ref, kept_q, queries), (k_ref, kept_k, keys), (v_ref, kept_v, values))
    ):
        rows[...] = x
        keeps.append(pltpu.make_async_copy(rows, place, begun_sem.at[requests + i]))
        keeps[-1].start()

    for h in range(heads):
        key = keys[:, FD * h : FD * (h + 1)]
        phi[h] = lined_phi(key, table_ref, bias_ref)
        plain[h] = plain_phi(key, table_ref, bias_ref)
        turned[h] = dot_nn(values[:, DV * h : DV * (h + 1)], table_ref[:DV, : PHASES * 128]).astype(BF16)

    column_width = tokens_ref.shape[1] // tp_size
    edge_rows = lax.broadcasted_iota(jnp.int32, (2 * requests, 24 * requests), 0)
    edge_columns = lax.broadcasted_iota(jnp.int32, (2 * requests, 24 * requests), 1)
    wanted = jnp.zeros(edge_rows.shape, jnp.int32)
    for r in range(requests):
        wanted = jnp.where(edge_rows // 2 == r, 24 * r + 6 + accepted_ref[r] + edge_rows % 2, wanted)
    choose = (edge_columns == wanted).astype(F32).astype(BF16)
    for i in range(tp_size):
        @pl.when(tp_here == i)
        def _():
            window = padded[:, column_width * i : column_width * (i + 1)].astype(BF16)
            edges[:, :column_width] = dot_nn(choose, window)

    lane_ids = lax.broadcasted_iota(jnp.int32, (LINES, 128), 1)
    step_ids = lax.broadcasted_iota(jnp.int32, (steps, 1), 0)
    edge_lines = -(-column_width // 128)
    for blank in blanks:
        blank.wait()
    sends = []
    for r in range(requests):
        owner = owner_ref[r]
        if r % 2 == 0:
            for load in loads[r // 2]:
                load.wait()
        taken = (step_ids < accepted_ref[r]).astype(F32)
        first, shift = line_of(r)
        extra[...] = jnp.zeros((EXTRA, 128), F32)
        for h in range(heads):
            rows = slice(steps * r, steps * (r + 1))
            spread_keys = spread((phi[h, rows, :] * taken).astype(BF16), table_ref)
            value_rows = turned[h, rows, :]
            parts = []
            for k in range(PHASES):
                block = value_rows[:, 128 * k : 128 * (k + 1)]
                early = one_line < DV - 16 * k
                zero = jnp.zeros((steps, 128), BF16)
                parts.append(jnp.where(early, block, zero))
                parts.append(jnp.where(early, zero, block))
            added = dot_tn(spread_keys, jnp.concatenate(parts, axis=0))[:LINES]
            start = flat[h, first : first + LINES, :]
            if shift:
                following = flat[h, first + 1 : first + 1 + LINES, :]
                start = pltpu.roll(jnp.where(lane_ids >= shift, start, following), 128 - shift, 1)
            begun[r, h] = start.astype(BF16)
            kept = start + added
            sums = jnp.sum(plain[h, rows, :] * taken, axis=0, keepdims=True)[:, :F] + norm_ref[h, r : r + 1, :]
            extra[2 * h : 2 * h + 1, :] = sums[:, :128]
            extra[2 * h + 1 : 2 * h + 2, :] = sums[:, 128:256]
            tail = jnp.concatenate([sums[:, 256:], jnp.zeros((1, 128 - (F - 256)), F32)], axis=1)
            stage[r, h * LINES : (h + 1) * LINES - 16, :] = kept[: LINES - 16].astype(BF16)
            stage[r, (h + 1) * LINES - 16 : (h + 1) * LINES, :] = jnp.where(
                one_row == 15, tail, kept[LINES - 16 :]
            ).astype(BF16)
        for j in range(2):
            for c in range(edge_lines):
                end = min(column_width, 128 * (c + 1))
                line = 2 * heads + edge_lines * j + c
                extra[line : line + 1, : end - 128 * c] = edges[2 * r + j : 2 * r + j + 1, 128 * c : end]
        marked = jnp.where(last & (one_line == 127), (owner + 1).astype(F32), extra[...] + count_mark)
        stage[r, body : body + EXTRA, :] = marked.astype(BF16)
        keep = pltpu.make_async_copy(begun.at[r], start_ref.at[r], begun_sem.at[r])
        keep.start()
        keeps.append(keep)
        if pair_cap == 1:
            routes = [(ranks[r] == 0, pieces[0].at[owner])]
        else:
            far = owner ^ lax.axis_index("req")
            routes = [((ranks[r] == 0) & (far == k), pieces[k].at[0]) for k in range(count)]
            routes += [(seconds[r], pieces[k].at[1]) for k in (0, 1, 2, 4)]
            routes += [(ranks[r] == 1, pieces[count].at[owner])]
        for i, (chosen, place) in enumerate(routes):
            send = pltpu.make_async_copy(stage.at[r], place, out_sem.at[r, i])
            sends.append((chosen, send))

            @pl.when(chosen)
            def _():
                send.start()
    for chosen, send in sends:
        @pl.when(chosen)
        def _():
            send.wait()
    for keep in keeps:
        keep.wait()


def attend_kernel(
    heads,
    q_ref, k_ref, v_ref, start_ref, norm_ref, wo_ref, table_ref, bias_ref,
    part_ref,
    attended,
):
    requests = start_ref.shape[0]
    rows_all = q_ref.shape[0]
    steps = rows_all // requests
    row_ids = lax.broadcasted_iota(jnp.int32, (rows_all, rows_all), 0)
    column_ids = lax.broadcasted_iota(jnp.int32, (rows_all, rows_all), 1)
    allowed = (row_ids // steps == column_ids // steps) & (row_ids >= column_ids)
    lane_ids = lax.broadcasted_iota(jnp.int32, (steps, 128), 1)
    for h in range(heads):
        query = q_ref[:, FD * h : FD * (h + 1)]
        key = k_ref[:, FD * h : FD * (h + 1)]
        value = v_ref[:, DV * h : DV * (h + 1)]
        phi = lined_phi(query, table_ref, bias_ref).astype(BF16)
        plain = plain_phi(query, table_ref, bias_ref)
        inner = dot_nt(query, key) * 0.25
        scores = jnp.where(allowed, 1.0 + inner + 0.5 * inner * inner, 0.0)
        below = jnp.sum(scores, axis=-1, keepdims=True)
        within = dot_nn(scores.astype(BF16), value)
        for r in range(requests):
            rows = slice(steps * r, steps * (r + 1))
            spread_query = spread(phi[rows], table_ref)[:, :LINES]
            lined = dot_nn(spread_query, start_ref[r, h])
            total = jnp.zeros((steps, 128), F32)
            for j in range(PHASES + 1):
                block = jnp.zeros((steps, 128), F32)
                if j < PHASES:
                    at = steps * (2 * j)
                    block = jnp.where(lane_ids < DV - 16 * j, lined[at : at + steps], 0.0)
                if j > 0:
                    at = steps * (2 * (j - 1) + 1)
                    block = jnp.where(lane_ids >= DV - 16 * (j - 1), lined[at : at + steps], block)
                total = total + (pltpu.roll(block, 16 * j, 1) if 0 < j < 8 else block)
            beneath = below[rows] + jnp.sum(plain[rows, :F] * norm_ref[h, r : r + 1, :], axis=-1, keepdims=True)
            attended[h, rows, :] = ((total[:, :DV] + within[rows]) / beneath).astype(BF16)
    out = dot_nn(attended[0], wo_ref[0:DV, :])
    for h in range(1, heads):
        out = out + dot_nn(attended[h], wo_ref[DV * h : DV * (h + 1), :])
    part_ref[...] = out.astype(BF16)


def mlp_kernel(tokens_ref, sum_ref, gain_ref, wg_ref, wu_ref, wd_ref, residual_ref, part_ref):
    residual = tokens_ref[...].astype(F32) + sum_ref[...].astype(F32)
    residual_ref[...] = residual
    mean = jnp.mean(residual * residual, axis=-1, keepdims=True)
    gain = gain_ref[...].reshape(1, gain_ref.shape[0])
    second = (residual * lax.rsqrt(mean + EPSILON) * gain).astype(BF16)
    gate = dot_nn(second, wg_ref[...])
    up = dot_nn(second, wu_ref[...])
    hidden = (gate / (1.0 + jnp.exp(-gate)) * up).astype(BF16)
    part_ref[...] = dot_nn(hidden, wd_ref[...]).astype(BF16)


def relay_kernel(across_ref, beside_ref, passed_ref, both_ref, sems):
    moves = [
        pltpu.make_async_copy(across_ref.at[1], passed_ref.at[0], sems.at[0]),
        pltpu.make_async_copy(across_ref.at[1], both_ref.at[0], sems.at[1]),
        pltpu.make_async_copy(beside_ref.at[1], both_ref.at[1], sems.at[2]),
    ]
    for move in moves:
        move.start()
    for move in moves:
        move.wait()


def close_kernel(residual_ref, sum_ref, *rest):
    marks, (out_ref, several_ref, lines, sems) = rest[:-4], rest[-4:]
    reads = [
        pltpu.make_async_copy(mark.at[0, pl.ds(mark.shape[1] - EXTRA, EXTRA)], lines.at[i], sems.at[i])
        for i, mark in enumerate(marks)
    ]
    for read in reads:
        read.start()
    out_ref[...] = (residual_ref[...] + sum_ref[...].astype(F32)).astype(BF16)
    for read in reads:
        read.wait()
    several_ref[0] = jnp.int32(0)
    if marks:
        row = lax.broadcasted_iota(jnp.int32, (EXTRA, 128), 0)
        lane = lax.broadcasted_iota(jnp.int32, (EXTRA, 128), 1)
        most = functools.reduce(jnp.maximum, [lines[i].astype(F32) for i in range(len(marks))])
        most = jnp.max(jnp.where((row == EXTRA - 1) & (lane == 126), most, 0.0))
        several_ref[0] = (most > 1.0).astype(jnp.int32)


def settle_kernel(heads, count, pair_cap, direct, arrivals, *rest):
    lanes = count * pair_cap
    body = heads * LINES
    here = lax.axis_index("req")
    inputs, rest = rest[:arrivals], rest[arrivals:]
    state_ref, norm_ref, edge_ref, stage, marks, flat, table, alive, in_sem, mark_sem, out_sem = rest
    loads, reads = [], []

    def load(place, lane):
        at = len(loads)
        loads.append(pltpu.make_async_copy(place, stage.at[lane], in_sem.at[lane]))
        reads.append(pltpu.make_async_copy(place.at[pl.ds(body, EXTRA)], marks.at[lane], mark_sem.at[at]))

    for i in range(count):
        if pair_cap == 1:
            load(inputs[0].at[i], i)
        else:
            source = here ^ i
            load(inputs[i].at[0], 2 * source)
            if direct:
                at, j = {3: (count, 1), 5: (count, 0), 6: (count + 1, 0), 7: (count + 2, 0)}.get(i, (i, 1))
                load(inputs[at].at[j], 2 * source + 1)
            else:
                load(inputs[count].at[i], 2 * i + 1)
    for copy in reads + loads:
        copy.start()
    norm_ref[...] = jnp.zeros(norm_ref.shape, F32)
    edge_ref[...] = jnp.zeros(edge_ref.shape, BF16)
    for copy in reads:
        copy.wait()
    one_row = lax.broadcasted_iota(jnp.int32, (EXTRA, 128), 0)
    one_line = lax.broadcasted_iota(jnp.int32, (EXTRA, 128), 1)
    mark = (one_row == EXTRA - 1) & (one_line == 127)
    filled = jnp.int32(0)
    for lane in range(lanes):
        block = jnp.where(mark, marks[lane].astype(F32), 0.0)
        live = (jnp.sum(block).astype(jnp.int32) == here + 1).astype(jnp.int32)
        table[filled] = lane
        alive[lane] = live
        filled = filled + live

    total = state_ref.shape[0]
    width = edge_ref.shape[2]
    edge_lines = -(-width // 128)
    lane_ids = lax.broadcasted_iota(jnp.int32, (LINES, 128), 1)
    head_ids = lax.broadcasted_iota(jnp.int32, (8, 128), 1)
    stores = []
    done = 0
    for s in range(CAP):
        first, shift = line_of(s)
        last = -(-((s + 1) * SPAN) // 128)
        span = last - first

        @pl.when(s < filled)
        def _():
            lane = table[s]
            pltpu.make_async_copy(stage.at[lane], stage.at[lane], in_sem.at[lane]).wait()
            extra = marks[lane].astype(F32)
            pairs = [[], []]
            for j in range(2):
                for c in range(edge_lines):
                    end = min(width, 128 * (c + 1))
                    line = 2 * heads + edge_lines * j + c
                    pairs[j].append(extra[line : line + 1, : end - 128 * c])
            edge_ref[s] = jnp.concatenate(
                [jnp.concatenate(pairs[j], axis=1) for j in range(2)], axis=0
            ).astype(BF16)
            for h in range(heads):
                rows = stage[lane, h * LINES : (h + 1) * LINES, :].astype(F32)
                norm_ref[h, s : s + 1, :] = jnp.concatenate(
                    [
                        extra[2 * h : 2 * h + 1, :],
                        extra[2 * h + 1 : 2 * h + 2, :],
                        rows[LINES - 1 : LINES, : F - 256],
                    ],
                    axis=1,
                )
                if shift:
                    rows = pltpu.roll(rows, shift, 1)
                    whole = span if span < LINES else LINES - 1
                    pltpu.store(flat.at[h, pl.ds(first, whole)], rows[:whole], mask=lane_ids[:whole] >= shift)
                    pltpu.store(flat.at[h, pl.ds(first + 1, span - 1)], rows[: span - 1], mask=lane_ids[: span - 1] < shift)
                else:
                    flat[h, first:last, :] = rows[:span]

        @pl.when(s >= filled)
        def _():
            for h in range(heads):
                if shift:
                    old = flat[h, first : first + 1, :]
                    flat[h, first + 1 : last, :] = jnp.zeros((span - 1, 128), F32)
                    flat[h, first : first + 1, :] = jnp.where(head_ids[:1] < shift, old, 0.0)
                else:
                    flat[h, first:last, :] = jnp.zeros((span, 128), F32)

        until = total if s == CAP - 1 else ((s + 1) * SPAN // 128) // 8 * 8
        for h in range(heads):
            store = pltpu.make_async_copy(
                flat.at[h, pl.ds(done, until - done)],
                state_ref.at[pl.ds(done, until - done), h],
                out_sem.at[s, h],
            )
            store.start()
            stores.append(store)
        done = until
    for lane in range(lanes):
        @pl.when(alive[lane] == 0)
        def _():
            pltpu.make_async_copy(stage.at[lane], stage.at[lane], in_sem.at[lane]).wait()
    for store in stores:
        store.wait()


def shards(
    tokens, conv_edge, state_start, norm_start, accepted, owner, attn_gain, conv_weight,
    w_query, w_key, w_value, w_out, mlp_gain, w_gate, w_up, w_down,
):
    requests, steps, width = tokens.shape
    count = lax.axis_size("req")
    tp_size = lax.axis_size("tp")
    pair_cap = (CAP + count - 1) // count
    heads = w_query.shape[1] // FD
    rows_all = requests * steps
    lines = state_start.shape[1] // 128
    payload = heads * LINES + EXTRA
    column_width = width // tp_size
    table, bias = (jnp.asarray(t) for t in tables())

    vmem = pl.BlockSpec(memory_space=pltpu.VMEM)
    smem = pl.BlockSpec(memory_space=pltpu.SMEM)
    hbm = pl.BlockSpec(memory_space=pltpu.HBM)
    anywhere = pl.BlockSpec(memory_space=pl.ANY)
    limit = functools.partial(pltpu.CompilerParams, vmem_limit_bytes=40 * 2**20)

    def cost(us):
        return pl.CostEstimate(flops=0, transcendentals=0, bytes_accessed=int(us * 3.6e2))

    flat_tokens = tokens.reshape(rows_all, width)
    lined_state = jnp.swapaxes(state_start.reshape(heads, lines, 128), 0, 1)
    held = [count] if pair_cap == 1 else [2, 2, 2, 1, 2, 1, 1, 1, count]
    piece_shapes = [jax.ShapeDtypeStruct((size, payload, 128), BF16) for size in held]
    fetched = [
        owner, accepted, flat_tokens, conv_edge, attn_gain, conv_weight,
        w_query.T, w_key.T, w_value, table, bias, norm_start,
    ]
    outs = pl.pallas_call(
        functools.partial(pack_kernel, heads, count, pair_cap, tp_size, len(fetched), len(held)),
        out_shape=piece_shapes
        + [
            jax.ShapeDtypeStruct((rows_all, heads * FD), BF16),
            jax.ShapeDtypeStruct((rows_all, heads * FD), BF16),
            jax.ShapeDtypeStruct((rows_all, heads * DV), BF16),
            jax.ShapeDtypeStruct((requests, heads, LINES, 128), BF16),
        ],
        in_specs=[hbm] * (1 + len(fetched)),
        out_specs=[anywhere] * (len(held) + 4),
        scratch_shapes=[pltpu.SMEM(x.shape, x.dtype) for x in fetched[:2]]
        + [pltpu.VMEM(x.shape, x.dtype) for x in fetched[2:]]
        + [
            pltpu.VMEM((heads, (lines + 1) // 8 * 8 + 8, 128), F32),
            pltpu.VMEM((requests * 24, width), F32),
            pltpu.VMEM((rows_all, width), BF16),
            pltpu.VMEM((heads, rows_all, 2 * WIDE), F32),
            pltpu.VMEM((heads, rows_all, 384), F32),
            pltpu.VMEM((heads, rows_all, PHASES * 128), BF16),
            pltpu.VMEM((2 * requests, -(-column_width // 128) * 128), F32),
            pltpu.VMEM((EXTRA, 128), F32),
            pltpu.VMEM((requests, payload, 128), BF16),
            pltpu.VMEM((requests, heads, LINES, 128), BF16),
            pltpu.VMEM((rows_all, heads * FD), BF16),
            pltpu.VMEM((rows_all, heads * FD), BF16),
            pltpu.VMEM((rows_all, heads * DV), BF16),
            pltpu.VMEM((EXTRA, 128), BF16),
            pltpu.SemaphoreType.DMA((requests // 2, heads)),
            pltpu.SemaphoreType.DMA((len(fetched),)),
            pltpu.SemaphoreType.DMA((sum(held),)),
            pltpu.SemaphoreType.DMA((requests, count + 6)),
            pltpu.SemaphoreType.DMA((requests + 3,)),
        ],
        compiler_params=limit(vmem_limit_bytes=60 * 2**20),
        cost_estimate=cost(8),
        name="pack",
    )(lined_state, *fetched)
    pieces, (queries, keys, values, start_rows) = list(outs[: len(held)]), outs[len(held) :]

    def swapped(x, far):
        return lax.ppermute(x, "req", [(i, i ^ far) for i in range(count)])

    arrived = {}

    def wave(now, fars, waits, later):
        for far in fars:
            arrived[far] = swapped(pieces[far], far)
        now, done, held_back = lax.optimization_barrier(
            (now, [arrived[far] for far in waits], [pieces[far] for far in later])
        )
        for far, x in zip(waits, done):
            arrived[far] = x
        for far, x in zip(later, held_back):
            pieces[far] = x
        return now

    cores = [[i, i + 1] for i in range(0, tp_size, 2)]
    chips = [list(range(core, tp_size, 2)) for core in range(2)]

    def summed(part, meet=lambda x: x):
        half = rows_all // 2
        both = lax.all_gather(part, "tp", axis=0, axis_index_groups=cores)
        mine = lax.dynamic_slice_in_dim(both, lax.axis_index("tp") % 2 * half, half, 1)
        mine = meet(jnp.sum(mine.astype(F32), axis=0).astype(BF16))
        mine = lax.all_gather(mine, "tp", axis=0, axis_index_groups=chips)
        mine = jnp.sum(mine.astype(F32), axis=0).astype(BF16)
        return lax.all_gather(mine, "tp", axis=0, tiled=True, axis_index_groups=cores)

    part = pl.pallas_call(
        functools.partial(attend_kernel, heads),
        out_shape=jax.ShapeDtypeStruct((rows_all, width), BF16),
        in_specs=[vmem] * 8,
        out_specs=vmem,
        scratch_shapes=[pltpu.VMEM((heads, rows_all, DV), BF16)],
        compiler_params=limit(),
        cost_estimate=cost(3),
        name="attend",
    )(
        queries, keys, values, start_rows, norm_start, w_out, table, bias,
    )
    total = summed(part)
    residual, part = pl.pallas_call(
        mlp_kernel,
        out_shape=[jax.ShapeDtypeStruct((rows_all, width), F32), jax.ShapeDtypeStruct((rows_all, width), BF16)],
        in_specs=[vmem] * 6,
        out_specs=[vmem] * 2,
        compiler_params=limit(),
        cost_estimate=cost(3),
        name="mlp",
    )(flat_tokens, total, mlp_gain, w_gate, w_up, w_down)
    forward = {}

    def half_way(x):
        if pair_cap > 1:
            x = wave(x, (4, 2, 1, 5, 3), (4, 2, 1, 5, 3), (6, 7))
            passed, both = pl.pallas_call(
                relay_kernel,
                out_shape=[jax.ShapeDtypeStruct((size, payload, 128), BF16) for size in (1, 2)],
                in_specs=[anywhere] * 2,
                out_specs=[anywhere] * 2,
                scratch_shapes=[pltpu.SemaphoreType.DMA((3,))],
                compiler_params=limit(),
                cost_estimate=cost(1),
                name="relay",
            )(arrived[4], arrived[2])
            forward.update({far: swapped(passed, far) for far in (2, 3)})
            forward[1] = swapped(both, 1)
        return x

    total = summed(part, half_way)
    if pair_cap > 1:
        total, forward = wave((total, forward), (6, 7), (6, 7), ())
    firsts, items = [], []
    if pair_cap > 1:
        arrived[0] = pieces[0]
        firsts = [arrived[far] for far in range(count)]
        items = [forward[far] for far in (1, 2, 3)]
    hidden_out, several = pl.pallas_call(
        close_kernel,
        out_shape=[jax.ShapeDtypeStruct((rows_all, width), BF16), jax.ShapeDtypeStruct((1,), jnp.int32)],
        in_specs=[vmem] * 2 + [anywhere] * len(firsts),
        out_specs=[vmem, smem],
        scratch_shapes=[pltpu.VMEM((count, EXTRA, 128), BF16), pltpu.SemaphoreType.DMA((count,))],
        compiler_params=limit(),
        cost_estimate=cost(1),
        name="close",
    )(residual, total, *firsts)

    out_lines = CAP * SPAN // 128

    def settled(direct, *inputs):
        return pl.pallas_call(
            functools.partial(settle_kernel, heads, count, pair_cap, direct, len(inputs)),
            out_shape=[
                jax.ShapeDtypeStruct((out_lines, heads, 128), F32),
                jax.ShapeDtypeStruct((heads, CAP, F), F32),
                jax.ShapeDtypeStruct((CAP, 2, column_width), BF16),
            ],
            in_specs=[anywhere] * len(inputs),
            out_specs=[anywhere, vmem, vmem],
            scratch_shapes=[
                pltpu.VMEM((count * pair_cap, payload, 128), BF16),
                pltpu.VMEM((count * pair_cap, EXTRA, 128), BF16),
                pltpu.VMEM((heads, out_lines, 128), F32),
                pltpu.SMEM((count * pair_cap + 1,), jnp.int32),
                pltpu.SMEM((count * pair_cap,), jnp.int32),
                pltpu.SemaphoreType.DMA((count * pair_cap,)),
                pltpu.SemaphoreType.DMA((count * pair_cap,)),
                pltpu.SemaphoreType.DMA((CAP, heads)),
            ],
            compiler_params=limit(),
            cost_estimate=cost(7),
            name="settle" if direct else "settle_general",
        )(*inputs)

    def exchanged(x):
        return lax.all_to_all(x, "req", 0, 0, tiled=True)

    if pair_cap > 1:
        kept_state, kept_norm, kept_edge = lax.cond(
            several[0] > 0,
            lambda firsts, items, spare: settled(False, *firsts, exchanged(spare)),
            lambda firsts, items, spare: settled(True, *firsts, *items),
            firsts, items, pieces[count],
        )
    else:
        kept_state, kept_norm, kept_edge = settled(True, exchanged(pieces[0]))
    return (
        hidden_out.reshape(requests, steps, width),
        jnp.swapaxes(kept_state, 0, 1).reshape(heads, out_lines * 128),
        kept_norm,
        kept_edge,
    )


def solution(mesh):
    placed = (
        P("req", None, None),
        P("req", None, None),
        P("tp", "req"),
        P("tp", "req", None),
        P("req"),
        P("req"),
        P(),
        P(),
        P(None, "tp"),
        P(None, "tp"),
        P("tp", None),
        P("tp", None),
        P(),
        P(None, "tp"),
        P(None, "tp"),
        P("tp", None),
    )
    return jax.shard_map(
        shards,
        mesh=mesh,
        in_specs=placed,
        out_specs=(
            P("req", None, None),
            P("tp", "req"),
            P("tp", "req", None),
            P("req", None, "tp"),
        ),
        check_vma=False,
    )
```

```python
import functools
import math

import jax
import jax.numpy as jnp
import numpy as np
from jax import lax
from jax.experimental import pallas as pl
from jax.experimental.pallas import tpu as pltpu
from jax.sharding import PartitionSpec as P

FD = 16
DV = 112
F = 273
CAP = 16
EPSILON = 1e-05

SPAN = F * DV
LINES = 240
WIDE = 256
PHASES = 7
EXTRA = 16
BF16 = jnp.bfloat16
F32 = jnp.float32


def line_of(index):
    return (index * SPAN) // 128, (index * SPAN) % 128


@functools.lru_cache(None)
def tables():
    scale_two = 0.25 * math.sqrt(0.5)

    def feature(column, f, left, right, bias):
        if f == 0:
            bias[0, column] = bias[1, column] = bias[2, column] = 1.0
        elif f <= FD:
            left[f - 1, column] = 1.0
            bias[1, column] = 1.0
            bias[2, column] = 0.5
        elif f < F:
            left[(f - 1 - FD) // FD, column] = 1.0
            right[(f - 1 - FD) % FD, column] = 1.0
            bias[2, column] = scale_two

    def build(width, places):
        left, right = np.zeros((FD, width)), np.zeros((FD, width))
        bias = np.zeros((8, width), np.float32)
        for column, f in places:
            feature(column, f, left, right, bias)
        return np.concatenate([left, right], 1).astype(BF16), bias

    lined = [
        (part * WIDE + m, 8 * (m // PHASES) + m % PHASES + part)
        for part in range(2)
        for m in range(LINES)
    ]
    line_pick, line_bias = build(2 * WIDE, lined)
    plain_pick, plain_bias = build(384, [(f, f) for f in range(F)])
    phase_mask = np.zeros((8, WIDE))
    for k in range(PHASES):
        phase_mask[k, k::PHASES] = 1.0
    turn = np.zeros((DV, PHASES * 128))
    for k in range(PHASES):
        for lane in range(128):
            turn[(16 * k + lane) % DV, 128 * k + lane] = 1.0
    table = np.zeros((DV + FD, 1792))
    table[:DV, : PHASES * 128] = turn
    table[:8, PHASES * 128 : PHASES * 128 + WIDE] = phase_mask
    table[DV:] = np.concatenate([line_pick, plain_pick], 1)
    return table.astype(BF16), np.concatenate([line_bias, plain_bias], 1)


def dot_nt(a, b):
    return lax.dot_general(a, b, (((1,), (1,)), ((), ())), preferred_element_type=F32)


def dot_tn(a, b):
    return lax.dot_general(a, b, (((0,), (0,)), ((), ())), preferred_element_type=F32)


def dot_nn(a, b):
    return jnp.dot(a, b, preferred_element_type=F32)


def expand(x, table_ref, bias_ref, start, width):
    both = dot_nn(x, table_ref[DV:, 2 * start : 2 * (start + width)])
    bias = bias_ref[:, start : start + width]
    left = both[:, :width] + bias[0:1, :]
    right = both[:, width:] + bias[1:2, :]
    return left * right * bias[2:3, :]


def lined_phi(x, table_ref, bias_ref):
    return expand(x, table_ref, bias_ref, 0, 2 * WIDE)


def plain_phi(x, table_ref, bias_ref):
    return expand(x, table_ref, bias_ref, 2 * WIDE, 384)


def spread(phi, table_ref):
    pieces = []
    for k in range(PHASES):
        chosen = table_ref[k : k + 1, PHASES * 128 : PHASES * 128 + WIDE]
        for part in range(2):
            pieces.append(phi[:, part * WIDE : (part + 1) * WIDE] * chosen)
    return jnp.concatenate(pieces, axis=0)


def pack_kernel(
    heads, count, pair_cap, tp_size, loaded, made,
    state_ref, *rest,
):
    fetched, rest = rest[:loaded], rest[loaded:]
    pieces, rest = rest[:made], rest[made:]
    (q_ref, k_ref, v_ref, start_ref), rest = rest[:4], rest[4:]
    held, rest = rest[:loaded], rest[loaded:]
    flat, padded, mixed, phi, plain, turned, edges, extra, stage, begun, kept_q, kept_k, kept_v, none, state_sem, load_sem, none_sem, out_sem, begun_sem = rest
    fetches = [pltpu.make_async_copy(fetched[i], held[i], load_sem.at[i]) for i in range(loaded)]
    for fetch in fetches:
        fetch.start()
    (
        owner_ref, accepted_ref, tokens_ref, edge_ref, gain_ref, conv_ref,
        wq_ref, wk_ref, wv_ref, table_ref, bias_ref, norm_ref,
    ) = held
    requests = owner_ref.shape[0]
    steps = tokens_ref.shape[0] // requests
    body = heads * LINES
    empty = [piece.at[i, pl.ds(body, EXTRA)] for piece in pieces for i in range(piece.shape[0])]
    blanks = [pltpu.make_async_copy(none, place, none_sem.at[i]) for i, place in enumerate(empty)]
    for fetch in fetches[:6]:
        fetch.wait()
    ranks, seconds, second = [], [], jnp.int32(0)
    for r in range(requests):
        rank = jnp.int32(0)
        for earlier in range(r):
            rank = rank + (owner_ref[earlier] == owner_ref[r]).astype(jnp.int32)
        ranks.append(rank)
        seconds.append((rank == 1) & (second == 0))
        second = second + (rank == 1).astype(jnp.int32)
    one_line = lax.broadcasted_iota(jnp.int32, (EXTRA, 128), 1)
    one_row = lax.broadcasted_iota(jnp.int32, (EXTRA, 128), 0)
    last = one_row == EXTRA - 1
    count_mark = jnp.where(last & (one_line == 126), second.astype(F32), 0.0)
    none[...] = count_mark.astype(BF16)
    for blank in blanks:
        blank.start()

    tp_here = lax.axis_index("tp")
    gain = gain_ref[...].reshape(1, gain_ref.shape[0])
    for r in range(requests):
        base = 24 * r
        wide = tokens_ref[steps * r : steps * (r + 1), :].astype(F32)
        mean = jnp.mean(wide * wide, axis=-1, keepdims=True)
        normed = (wide * lax.rsqrt(mean + EPSILON) * gain).astype(BF16).astype(F32)
        padded[base + 8 : base + 8 + steps, :] = normed
        padded[base : base + 8, :] = jnp.zeros((8, wide.shape[1]), F32)
        padded[base + 6 : base + 8, :] = edge_ref[r].astype(F32)
        convolved = conv_ref[2:3, :] * normed
        for tap in range(2):
            convolved = convolved + conv_ref[tap : tap + 1, :] * padded[base + 6 + tap : base + 6 + tap + steps, :]
        blend = normed + convolved / (1.0 + jnp.exp(-normed))
        mixed[steps * r : steps * (r + 1), :] = blend.astype(BF16)

    lines = state_ref.shape[0]
    cuts = [0] + [-(-(line_of(r)[0] + 3) // 8) * 8 for r in range(2, requests, 2)] + [lines]
    loads = [
        [
            pltpu.make_async_copy(
                state_ref.at[pl.ds(begin, end - begin), h], flat.at[h, pl.ds(begin, end - begin)], state_sem.at[i, h]
            )
            for h in range(heads)
        ]
        for i, (begin, end) in enumerate(zip(cuts, cuts[1:]))
    ]
    for part in loads:
        for load in part:
            load.start()
    for fetch in fetches[6:]:
        fetch.wait()
    queries = dot_nt(mixed[...], wq_ref[...]).astype(BF16)
    keys = dot_nt(mixed[...], wk_ref[...]).astype(BF16)
    values = dot_nt(mixed[...], wv_ref[...]).astype(BF16)
    keeps = []
    for i, (place, rows, x) in enumerate(
        ((q_ref, kept_q, queries), (k_ref, kept_k, keys), (v_ref, kept_v, values))
    ):
        rows[...] = x
        keeps.append(pltpu.make_async_copy(rows, place, begun_sem.at[requests + i]))
        keeps[-1].start()

    for h in range(heads):
        key = keys[:, FD * h : FD * (h + 1)]
        phi[h] = lined_phi(key, table_ref, bias_ref)
        plain[h] = plain_phi(key, table_ref, bias_ref)
        turned[h] = dot_nn(values[:, DV * h : DV * (h + 1)], table_ref[:DV, : PHASES * 128]).astype(BF16)

    column_width = tokens_ref.shape[1] // tp_size
    edge_rows = lax.broadcasted_iota(jnp.int32, (2 * requests, 24 * requests), 0)
    edge_columns = lax.broadcasted_iota(jnp.int32, (2 * requests, 24 * requests), 1)
    wanted = jnp.zeros(edge_rows.shape, jnp.int32)
    for r in range(requests):
        wanted = jnp.where(edge_rows // 2 == r, 24 * r + 6 + accepted_ref[r] + edge_rows % 2, wanted)
    choose = (edge_columns == wanted).astype(F32).astype(BF16)
    for i in range(tp_size):
        @pl.when(tp_here == i)
        def _():
            window = padded[:, column_width * i : column_width * (i + 1)].astype(BF16)
            edges[:, :column_width] = dot_nn(choose, window)

    lane_ids = lax.broadcasted_iota(jnp.int32, (LINES, 128), 1)
    step_ids = lax.broadcasted_iota(jnp.int32, (steps, 1), 0)
    edge_lines = -(-column_width // 128)
    for blank in blanks:
        blank.wait()
    sends = []
    for r in range(requests):
        owner = owner_ref[r]
        if r % 2 == 0:
            for load in loads[r // 2]:
                load.wait()
        taken = (step_ids < accepted_ref[r]).astype(F32)
        first, shift = line_of(r)
        extra[...] = jnp.zeros((EXTRA, 128), F32)
        for h in range(heads):
            rows = slice(steps * r, steps * (r + 1))
            spread_keys = spread((phi[h, rows, :] * taken).astype(BF16), table_ref)
            value_rows = turned[h, rows, :]
            parts = []
            for k in range(PHASES):
                block = value_rows[:, 128 * k : 128 * (k + 1)]
                early = one_line < DV - 16 * k
                zero = jnp.zeros((steps, 128), BF16)
                parts.append(jnp.where(early, block, zero))
                parts.append(jnp.where(early, zero, block))
            added = dot_tn(spread_keys, jnp.concatenate(parts, axis=0))[:LINES]
            start = flat[h, first : first + LINES, :]
            if shift:
                following = flat[h, first + 1 : first + 1 + LINES, :]
                start = pltpu.roll(jnp.where(lane_ids >= shift, start, following), 128 - shift, 1)
            begun[r, h] = start.astype(BF16)
            kept = start + added
            sums = jnp.sum(plain[h, rows, :] * taken, axis=0, keepdims=True)[:, :F] + norm_ref[h, r : r + 1, :]
            extra[2 * h : 2 * h + 1, :] = sums[:, :128]
            extra[2 * h + 1 : 2 * h + 2, :] = sums[:, 128:256]
            tail = jnp.concatenate([sums[:, 256:], jnp.zeros((1, 128 - (F - 256)), F32)], axis=1)
            stage[r, h * LINES : (h + 1) * LINES - 16, :] = kept[: LINES - 16].astype(BF16)
            stage[r, (h + 1) * LINES - 16 : (h + 1) * LINES, :] = jnp.where(
                one_row == 15, tail, kept[LINES - 16 :]
            ).astype(BF16)
        for j in range(2):
            for c in range(edge_lines):
                end = min(column_width, 128 * (c + 1))
                line = 2 * heads + edge_lines * j + c
                extra[line : line + 1, : end - 128 * c] = edges[2 * r + j : 2 * r + j + 1, 128 * c : end]
        marked = jnp.where(last & (one_line == 127), (owner + 1).astype(F32), extra[...] + count_mark)
        stage[r, body : body + EXTRA, :] = marked.astype(BF16)
        keep = pltpu.make_async_copy(begun.at[r], start_ref.at[r], begun_sem.at[r])
        keep.start()
        keeps.append(keep)
        if pair_cap == 1:
            routes = [(ranks[r] == 0, pieces[0].at[owner])]
        else:
            far = owner ^ lax.axis_index("req")
            routes = [((ranks[r] == 0) & (far == k), pieces[k].at[0]) for k in range(count)]
            routes += [(seconds[r], pieces[k].at[1]) for k in (0, 1, 2, 4)]
            routes += [(ranks[r] == 1, pieces[count].at[owner])]
        for i, (chosen, place) in enumerate(routes):
            send = pltpu.make_async_copy(stage.at[r], place, out_sem.at[r, i])
            sends.append((chosen, send))

            @pl.when(chosen)
            def _():
                send.start()
    for chosen, send in sends:
        @pl.when(chosen)
        def _():
            send.wait()
    for keep in keeps:
        keep.wait()


def attend_kernel(
    heads,
    q_ref, k_ref, v_ref, start_ref, norm_ref, wo_ref, table_ref, bias_ref,
    part_ref,
    attended,
):
    requests = start_ref.shape[0]
    rows_all = q_ref.shape[0]
    steps = rows_all // requests
    row_ids = lax.broadcasted_iota(jnp.int32, (rows_all, rows_all), 0)
    column_ids = lax.broadcasted_iota(jnp.int32, (rows_all, rows_all), 1)
    allowed = (row_ids // steps == column_ids // steps) & (row_ids >= column_ids)
    lane_ids = lax.broadcasted_iota(jnp.int32, (steps, 128), 1)
    for h in range(heads):
        query = q_ref[:, FD * h : FD * (h + 1)]
        key = k_ref[:, FD * h : FD * (h + 1)]
        value = v_ref[:, DV * h : DV * (h + 1)]
        phi = lined_phi(query, table_ref, bias_ref).astype(BF16)
        plain = plain_phi(query, table_ref, bias_ref)
        inner = dot_nt(query, key) * 0.25
        scores = jnp.where(allowed, 1.0 + inner + 0.5 * inner * inner, 0.0)
        below = jnp.sum(scores, axis=-1, keepdims=True)
        within = dot_nn(scores.astype(BF16), value)
        for r in range(requests):
            rows = slice(steps * r, steps * (r + 1))
            spread_query = spread(phi[rows], table_ref)[:, :LINES]
            lined = dot_nn(spread_query, start_ref[r, h])
            total = jnp.zeros((steps, 128), F32)
            for j in range(PHASES + 1):
                block = jnp.zeros((steps, 128), F32)
                if j < PHASES:
                    at = steps * (2 * j)
                    block = jnp.where(lane_ids < DV - 16 * j, lined[at : at + steps], 0.0)
                if j > 0:
                    at = steps * (2 * (j - 1) + 1)
                    block = jnp.where(lane_ids >= DV - 16 * (j - 1), lined[at : at + steps], block)
                total = total + (pltpu.roll(block, 16 * j, 1) if 0 < j < 8 else block)
            beneath = below[rows] + jnp.sum(plain[rows, :F] * norm_ref[h, r : r + 1, :], axis=-1, keepdims=True)
            attended[h, rows, :] = ((total[:, :DV] + within[rows]) / beneath).astype(BF16)
    out = dot_nn(attended[0], wo_ref[0:DV, :])
    for h in range(1, heads):
        out = out + dot_nn(attended[h], wo_ref[DV * h : DV * (h + 1), :])
    part_ref[...] = out.astype(BF16)


def mlp_kernel(tokens_ref, sum_ref, gain_ref, wg_ref, wu_ref, wd_ref, residual_ref, part_ref):
    residual = tokens_ref[...].astype(F32) + sum_ref[...].astype(F32)
    residual_ref[...] = residual
    mean = jnp.mean(residual * residual, axis=-1, keepdims=True)
    gain = gain_ref[...].reshape(1, gain_ref.shape[0])
    second = (residual * lax.rsqrt(mean + EPSILON) * gain).astype(BF16)
    gate = dot_nn(second, wg_ref[...])
    up = dot_nn(second, wu_ref[...])
    hidden = (gate / (1.0 + jnp.exp(-gate)) * up).astype(BF16)
    part_ref[...] = dot_nn(hidden, wd_ref[...]).astype(BF16)


def relay_kernel(across_ref, beside_ref, passed_ref, both_ref, sems):
    moves = [
        pltpu.make_async_copy(across_ref.at[1], passed_ref.at[0], sems.at[0]),
        pltpu.make_async_copy(across_ref.at[1], both_ref.at[0], sems.at[1]),
        pltpu.make_async_copy(beside_ref.at[1], both_ref.at[1], sems.at[2]),
    ]
    for move in moves:
        move.start()
    for move in moves:
        move.wait()


def close_kernel(residual_ref, sum_ref, *rest):
    marks, (out_ref, several_ref, lines, sems) = rest[:-4], rest[-4:]
    reads = [
        pltpu.make_async_copy(mark.at[0, pl.ds(mark.shape[1] - EXTRA, EXTRA)], lines.at[i], sems.at[i])
        for i, mark in enumerate(marks)
    ]
    for read in reads:
        read.start()
    out_ref[...] = (residual_ref[...] + sum_ref[...].astype(F32)).astype(BF16)
    for read in reads:
        read.wait()
    several_ref[0] = jnp.int32(0)
    if marks:
        row = lax.broadcasted_iota(jnp.int32, (EXTRA, 128), 0)
        lane = lax.broadcasted_iota(jnp.int32, (EXTRA, 128), 1)
        most = functools.reduce(jnp.maximum, [lines[i].astype(F32) for i in range(len(marks))])
        most = jnp.max(jnp.where((row == EXTRA - 1) & (lane == 126), most, 0.0))
        several_ref[0] = (most > 1.0).astype(jnp.int32)


def settle_kernel(heads, count, pair_cap, direct, arrivals, *rest):
    lanes = count * pair_cap
    body = heads * LINES
    here = lax.axis_index("req")
    inputs, rest = rest[:arrivals], rest[arrivals:]
    state_ref, norm_ref, edge_ref, stage, marks, flat, table, alive, in_sem, mark_sem, out_sem = rest
    loads, reads = [], []

    def load(place, lane):
        at = len(loads)
        loads.append(pltpu.make_async_copy(place, stage.at[lane], in_sem.at[lane]))
        reads.append(pltpu.make_async_copy(place.at[pl.ds(body, EXTRA)], marks.at[lane], mark_sem.at[at]))

    for i in range(count):
        if pair_cap == 1:
            load(inputs[0].at[i], i)
        else:
            source = here ^ i
            load(inputs[i].at[0], 2 * source)
            if direct:
                at, j = {3: (count, 1), 5: (count, 0), 6: (count + 1, 0), 7: (count + 2, 0)}.get(i, (i, 1))
                load(inputs[at].at[j], 2 * source + 1)
            else:
                load(inputs[count].at[i], 2 * i + 1)
    for copy in reads + loads:
        copy.start()
    norm_ref[...] = jnp.zeros(norm_ref.shape, F32)
    edge_ref[...] = jnp.zeros(edge_ref.shape, BF16)
    for copy in reads:
        copy.wait()
    one_row = lax.broadcasted_iota(jnp.int32, (EXTRA, 128), 0)
    one_line = lax.broadcasted_iota(jnp.int32, (EXTRA, 128), 1)
    mark = (one_row == EXTRA - 1) & (one_line == 127)
    filled = jnp.int32(0)
    for lane in range(lanes):
        block = jnp.where(mark, marks[lane].astype(F32), 0.0)
        live = (jnp.sum(block).astype(jnp.int32) == here + 1).astype(jnp.int32)
        table[filled] = lane
        alive[lane] = live
        filled = filled + live

    total = state_ref.shape[0]
    width = edge_ref.shape[2]
    edge_lines = -(-width // 128)
    lane_ids = lax.broadcasted_iota(jnp.int32, (LINES, 128), 1)
    head_ids = lax.broadcasted_iota(jnp.int32, (8, 128), 1)
    stores = []
    done = 0
    for s in range(CAP):
        first, shift = line_of(s)
        last = -(-((s + 1) * SPAN) // 128)
        span = last - first

        @pl.when(s < filled)
        def _():
            lane = table[s]
            pltpu.make_async_copy(stage.at[lane], stage.at[lane], in_sem.at[lane]).wait()
            extra = marks[lane].astype(F32)
            pairs = [[], []]
            for j in range(2):
                for c in range(edge_lines):
                    end = min(width, 128 * (c + 1))
                    line = 2 * heads + edge_lines * j + c
                    pairs[j].append(extra[line : line + 1, : end - 128 * c])
            edge_ref[s] = jnp.concatenate(
                [jnp.concatenate(pairs[j], axis=1) for j in range(2)], axis=0
            ).astype(BF16)
            for h in range(heads):
                rows = stage[lane, h * LINES : (h + 1) * LINES, :].astype(F32)
                norm_ref[h, s : s + 1, :] = jnp.concatenate(
                    [
                        extra[2 * h : 2 * h + 1, :],
                        extra[2 * h + 1 : 2 * h + 2, :],
                        rows[LINES - 1 : LINES, : F - 256],
                    ],
                    axis=1,
                )
                if shift:
                    rows = pltpu.roll(rows, shift, 1)
                    whole = span if span < LINES else LINES - 1
                    pltpu.store(flat.at[h, pl.ds(first, whole)], rows[:whole], mask=lane_ids[:whole] >= shift)
                    pltpu.store(flat.at[h, pl.ds(first + 1, span - 1)], rows[: span - 1], mask=lane_ids[: span - 1] < shift)
                else:
                    flat[h, first:last, :] = rows[:span]

        @pl.when(s >= filled)
        def _():
            for h in range(heads):
                if shift:
                    old = flat[h, first : first + 1, :]
                    flat[h, first + 1 : last, :] = jnp.zeros((span - 1, 128), F32)
                    flat[h, first : first + 1, :] = jnp.where(head_ids[:1] < shift, old, 0.0)
                else:
                    flat[h, first:last, :] = jnp.zeros((span, 128), F32)

        until = total if s == CAP - 1 else ((s + 1) * SPAN // 128) // 8 * 8
        for h in range(heads):
            store = pltpu.make_async_copy(
                flat.at[h, pl.ds(done, until - done)],
                state_ref.at[pl.ds(done, until - done), h],
                out_sem.at[s, h],
            )
            store.start()
            stores.append(store)
        done = until
    for lane in range(lanes):
        @pl.when(alive[lane] == 0)
        def _():
            pltpu.make_async_copy(stage.at[lane], stage.at[lane], in_sem.at[lane]).wait()
    for store in stores:
        store.wait()


def shards(
    tokens, conv_edge, state_start, norm_start, accepted, owner, attn_gain, conv_weight,
    w_query, w_key, w_value, w_out, mlp_gain, w_gate, w_up, w_down,
):
    requests, steps, width = tokens.shape
    count = lax.axis_size("req")
    tp_size = lax.axis_size("tp")
    pair_cap = (CAP + count - 1) // count
    heads = w_query.shape[1] // FD
    rows_all = requests * steps
    lines = state_start.shape[1] // 128
    payload = heads * LINES + EXTRA
    column_width = width // tp_size
    table, bias = (jnp.asarray(t) for t in tables())

    vmem = pl.BlockSpec(memory_space=pltpu.VMEM)
    smem = pl.BlockSpec(memory_space=pltpu.SMEM)
    hbm = pl.BlockSpec(memory_space=pltpu.HBM)
    anywhere = pl.BlockSpec(memory_space=pl.ANY)
    limit = functools.partial(pltpu.CompilerParams, vmem_limit_bytes=40 * 2**20)

    def cost(us):
        return pl.CostEstimate(flops=0, transcendentals=0, bytes_accessed=int(us * 3.6e2))

    flat_tokens = tokens.reshape(rows_all, width)
    lined_state = jnp.swapaxes(state_start.reshape(heads, lines, 128), 0, 1)
    held = [count] if pair_cap == 1 else [2, 2, 2, 1, 2, 1, 1, 1, count]
    piece_shapes = [jax.ShapeDtypeStruct((size, payload, 128), BF16) for size in held]
    fetched = [
        owner, accepted, flat_tokens, conv_edge, attn_gain, conv_weight,
        w_query.T, w_key.T, w_value, table, bias, norm_start,
    ]
    outs = pl.pallas_call(
        functools.partial(pack_kernel, heads, count, pair_cap, tp_size, len(fetched), len(held)),
        out_shape=piece_shapes
        + [
            jax.ShapeDtypeStruct((rows_all, heads * FD), BF16),
            jax.ShapeDtypeStruct((rows_all, heads * FD), BF16),
            jax.ShapeDtypeStruct((rows_all, heads * DV), BF16),
            jax.ShapeDtypeStruct((requests, heads, LINES, 128), BF16),
        ],
        in_specs=[hbm] * (1 + len(fetched)),
        out_specs=[anywhere] * (len(held) + 4),
        scratch_shapes=[pltpu.SMEM(x.shape, x.dtype) for x in fetched[:2]]
        + [pltpu.VMEM(x.shape, x.dtype) for x in fetched[2:]]
        + [
            pltpu.VMEM((heads, (lines + 1) // 8 * 8 + 8, 128), F32),
            pltpu.VMEM((requests * 24, width), F32),
            pltpu.VMEM((rows_all, width), BF16),
            pltpu.VMEM((heads, rows_all, 2 * WIDE), F32),
            pltpu.VMEM((heads, rows_all, 384), F32),
            pltpu.VMEM((heads, rows_all, PHASES * 128), BF16),
            pltpu.VMEM((2 * requests, -(-column_width // 128) * 128), F32),
            pltpu.VMEM((EXTRA, 128), F32),
            pltpu.VMEM((requests, payload, 128), BF16),
            pltpu.VMEM((requests, heads, LINES, 128), BF16),
            pltpu.VMEM((rows_all, heads * FD), BF16),
            pltpu.VMEM((rows_all, heads * FD), BF16),
            pltpu.VMEM((rows_all, heads * DV), BF16),
            pltpu.VMEM((EXTRA, 128), BF16),
            pltpu.SemaphoreType.DMA((requests // 2, heads)),
            pltpu.SemaphoreType.DMA((len(fetched),)),
            pltpu.SemaphoreType.DMA((sum(held),)),
            pltpu.SemaphoreType.DMA((requests, count + 6)),
            pltpu.SemaphoreType.DMA((requests + 3,)),
        ],
        compiler_params=limit(vmem_limit_bytes=60 * 2**20),
        cost_estimate=cost(8),
        name="pack",
    )(lined_state, *fetched)
    pieces, (queries, keys, values, start_rows) = list(outs[: len(held)]), outs[len(held) :]

    def swapped(x, far):
        return lax.ppermute(x, "req", [(i, i ^ far) for i in range(count)])

    arrived = {}

    def wave(now, fars, waits, later):
        for far in fars:
            arrived[far] = swapped(pieces[far], far)
        now, done, held_back = lax.optimization_barrier(
            (now, [arrived[far] for far in waits], [pieces[far] for far in later])
        )
        for far, x in zip(waits, done):
            arrived[far] = x
        for far, x in zip(later, held_back):
            pieces[far] = x
        return now

    cores = [[i, i + 1] for i in range(0, tp_size, 2)]
    chips = [list(range(core, tp_size, 2)) for core in range(2)]

    def summed(part, meet=lambda x: x):
        half = rows_all // 2
        both = lax.all_gather(part, "tp", axis=0, axis_index_groups=cores)
        mine = lax.dynamic_slice_in_dim(both, lax.axis_index("tp") % 2 * half, half, 1)
        mine = meet(jnp.sum(mine.astype(F32), axis=0).astype(BF16))
        mine = lax.all_gather(mine, "tp", axis=0, axis_index_groups=chips)
        mine = jnp.sum(mine.astype(F32), axis=0).astype(BF16)
        return lax.all_gather(mine, "tp", axis=0, tiled=True, axis_index_groups=cores)

    part = pl.pallas_call(
        functools.partial(attend_kernel, heads),
        out_shape=jax.ShapeDtypeStruct((rows_all, width), BF16),
        in_specs=[vmem] * 8,
        out_specs=vmem,
        scratch_shapes=[pltpu.VMEM((heads, rows_all, DV), BF16)],
        compiler_params=limit(),
        cost_estimate=cost(3),
        name="attend",
    )(
        queries, keys, values, start_rows, norm_start, w_out, table, bias,
    )
    total = summed(part)
    residual, part = pl.pallas_call(
        mlp_kernel,
        out_shape=[jax.ShapeDtypeStruct((rows_all, width), F32), jax.ShapeDtypeStruct((rows_all, width), BF16)],
        in_specs=[vmem] * 6,
        out_specs=[vmem] * 2,
        compiler_params=limit(),
        cost_estimate=cost(3),
        name="mlp",
    )(flat_tokens, total, mlp_gain, w_gate, w_up, w_down)
    forward = {}

    def half_way(x):
        if pair_cap > 1:
            x = wave(x, (4, 2, 1, 5, 3), (4, 2, 1, 5, 3), (6, 7))
            passed, both = pl.pallas_call(
                relay_kernel,
                out_shape=[jax.ShapeDtypeStruct((size, payload, 128), BF16) for size in (1, 2)],
                in_specs=[anywhere] * 2,
                out_specs=[anywhere] * 2,
                scratch_shapes=[pltpu.SemaphoreType.DMA((3,))],
                compiler_params=limit(),
                cost_estimate=cost(1),
                name="relay",
            )(arrived[4], arrived[2])
            forward[1] = swapped(both, 1)
            forward.update({far: swapped(passed, far) for far in (3, 2)})
        return x

    total = summed(part, half_way)
    if pair_cap > 1:
        total = wave(total, (6, 7), (6, 7), ())
    firsts, items = [], []
    if pair_cap > 1:
        arrived[0] = pieces[0]
        firsts = [arrived[far] for far in range(count)]
        items = [forward[far] for far in (1, 2, 3)]
    hidden_out, several = pl.pallas_call(
        close_kernel,
        out_shape=[jax.ShapeDtypeStruct((rows_all, width), BF16), jax.ShapeDtypeStruct((1,), jnp.int32)],
        in_specs=[vmem] * 2 + [anywhere] * len(firsts),
        out_specs=[vmem, smem],
        scratch_shapes=[pltpu.VMEM((count, EXTRA, 128), BF16), pltpu.SemaphoreType.DMA((count,))],
        compiler_params=limit(),
        cost_estimate=cost(1),
        name="close",
    )(residual, total, *firsts)

    out_lines = CAP * SPAN // 128

    def settled(direct, *inputs):
        return pl.pallas_call(
            functools.partial(settle_kernel, heads, count, pair_cap, direct, len(inputs)),
            out_shape=[
                jax.ShapeDtypeStruct((out_lines, heads, 128), F32),
                jax.ShapeDtypeStruct((heads, CAP, F), F32),
                jax.ShapeDtypeStruct((CAP, 2, column_width), BF16),
            ],
            in_specs=[anywhere] * len(inputs),
            out_specs=[anywhere, vmem, vmem],
            scratch_shapes=[
                pltpu.VMEM((count * pair_cap, payload, 128), BF16),
                pltpu.VMEM((count * pair_cap, EXTRA, 128), BF16),
                pltpu.VMEM((heads, out_lines, 128), F32),
                pltpu.SMEM((count * pair_cap + 1,), jnp.int32),
                pltpu.SMEM((count * pair_cap,), jnp.int32),
                pltpu.SemaphoreType.DMA((count * pair_cap,)),
                pltpu.SemaphoreType.DMA((count * pair_cap,)),
                pltpu.SemaphoreType.DMA((CAP, heads)),
            ],
            compiler_params=limit(),
            cost_estimate=cost(7),
            name="settle" if direct else "settle_general",
        )(*inputs)

    def exchanged(x):
        return lax.all_to_all(x, "req", 0, 0, tiled=True)

    if pair_cap > 1:
        kept_state, kept_norm, kept_edge = lax.cond(
            several[0] > 0,
            lambda firsts, items, spare: settled(False, *firsts, exchanged(spare)),
            lambda firsts, items, spare: settled(True, *firsts, *items),
            firsts, items, pieces[count],
        )
    else:
        kept_state, kept_norm, kept_edge = settled(True, exchanged(pieces[0]))
    return (
        hidden_out.reshape(requests, steps, width),
        jnp.swapaxes(kept_state, 0, 1).reshape(heads, out_lines * 128),
        kept_norm,
        kept_edge,
    )


def solution(mesh):
    placed = (
        P("req", None, None),
        P("req", None, None),
        P("tp", "req"),
        P("tp", "req", None),
        P("req"),
        P("req"),
        P(),
        P(),
        P(None, "tp"),
        P(None, "tp"),
        P("tp", None),
        P("tp", None),
        P(),
        P(None, "tp"),
        P(None, "tp"),
        P("tp", None),
    )
    return jax.shard_map(
        shards,
        mesh=mesh,
        in_specs=placed,
        out_specs=(
            P("req", None, None),
            P("tp", "req"),
            P("tp", "req", None),
            P("req", None, "tp"),
        ),
        check_vma=False,
    )
```
